32 devices in a mesh: dp: 16 (over z, x, core), tp: 2 (over y).
Axes of the slice: x: 2, y: 2, z: 4, core: 2. Of those that a mesh axis runs over, the one named last changes fastest.
Arguments:
- block_input: bfloat16 [16384, 768], P('dp'), may hold values from -6 to 6
- segment_ids: int32 [16384], P('dp'), may hold values from 0 to 79, never falling along the last dimension, each value on 1 to 256 neighbouring positions
- gain_one: float32 [768], replicated, may hold values from 0.5 to 1.5
- shift_one: float32 [768], replicated, may hold values from -3 to 3
- qkv_weight: bfloat16 [768, 3, 768], P(None, None, 'tp'), may hold values from -0.21875 to 0.21875
- out_weight: bfloat16 [768, 768], P('tp'), may hold values from -1.25 to 1.25
- gain_two: float32 [768], replicated, may hold values from 0.5 to 1.5
- shift_two: float32 [768], replicated, may hold values from -3 to 3
- up_weight: bfloat16 [768, 3072], P(None, 'tp'), may hold values from -0.21875 to 0.21875
- down_weight: bfloat16 [3072, 768], P('tp'), may hold values from -0.109375 to 0.109375
- out_cotangent: bfloat16 [16384, 768], P('dp'), may hold values from -6 to 6
Outputs:
- block_output: bfloat16 [16384, 768], P('dp')
- input_grad: bfloat16 [16384, 768], P('dp')
- qkv_grad: float32 [768, 3, 768], P('dp', None, 'tp')
- proj_grad: float32 [768, 768], P('tp', 'dp')
- up_grad: float32 [768, 3072], P('dp', 'tp')
- down_grad: float32 [3072, 768], P('tp', 'dp')
- norm_grads: float32 [4, 768], P(None, 'dp')
The draws below stay inside these ranges and needn't reach their ends.
Inputs may be any that keep to these rules, and one draw needn't show every extreme that they name: `segment_ids`: segment numbers never fall along the tokens; each segment holds 1 to 256 tokens and some segment exactly 256; a segment that crosses the end of a sequence is cut there by the sequence bound.
All inputs are finite; a program needn't handle non-finite values.
Results may differ from the reference program's by a relative error of at most 0.0095.
Values may be sent and summed in bfloat16 or wider, within the bound.
A program may use at most 128 MiB of HBM per device.

```python
import math
import jax
import jax.numpy as jnp
import numpy as np
from jax import lax

D = 768
H = 16
HD = 48
FF = 3072
SEQ = 1024
IMG = 256
TOKENS = 16384


def strengthened(drawn, rng, source, target, shards_of, factor):
    owner, partner = [(jnp.arange(drawn.shape[position]) // (drawn.shape[position] // shards_of)).reshape([-1 if axis == position else 1 for axis in range(drawn.ndim)]) for position in (source, target)]
    chosen = jax.random.permutation(rng, shards_of)[partner]
    strong = (owner == chosen) | (owner == (partner + shards_of // 2) % shards_of)
    return jnp.where(strong, factor * drawn, drawn)


def levels(key, dims, shards, smallest, top_value):
    loudness, own = 1.0, jax.random.fold_in(key, 6)
    for position, parts in shards:
        steps = jnp.exp(jax.random.uniform(jax.random.fold_in(own, position), (parts,), jnp.float32, smallest / len(shards), top_value / len(shards)))
        loudness = loudness * jnp.repeat(steps, dims[position] // parts).reshape([-1 if axis == position else 1 for axis in range(len(dims))])
    return loudness


def split_up(amount, total, bound, slope):
    weights = [(1 << 20) // math.isqrt(grade ** slope) + 1 for grade in range(2, amount + 1)]
    rest, given = total - bound - (amount - 1), [1] * (amount - 1)
    while rest > 0:
        free = [i for i in range(amount - 1) if given[i] < bound]
        mass, remaining = sum([weights[i] for i in free]), rest
        for i in free:
            addition = min(bound - given[i], max(1, remaining * weights[i] // mass), rest)
            given[i] = given[i] + addition
            rest = rest - addition
    return np.array([bound] + given)


def uneven(stream_key, count, total, limit, lean):
    if count == 2:
        one = jax.random.randint(stream_key, (), max(1, total - limit), min(limit, total - 1) + 1)
        return jnp.stack([one, total - one])
    sizes = jnp.asarray(split_up(count, total, limit, lean), jnp.int32)
    twos = (count - 1) // 2
    giver, receiver = sizes[1:1 + 2 * twos:2], sizes[2:2 + 2 * twos:2]
    room = jnp.minimum(giver - 1, limit - receiver)
    shifted = jax.random.randint(jax.random.fold_in(stream_key, 1), (twos,), 0, 1 << 20) % (room + 1)
    sizes = sizes.at[1:1 + 2 * twos:2].set(giver - shifted).at[2:2 + 2 * twos:2].set(receiver + shifted)
    return sizes[jax.random.permutation(jax.random.fold_in(stream_key, 2), count)]


def normal_values(stream_key, dims, width, most, shards=(), kind=jnp.bfloat16):
    array = width * jax.random.normal(stream_key, dims, jnp.float32)
    if shards:
        array = array * levels(stream_key, dims, shards, -0.22, 0.18)
    return jnp.clip(array, -most, most).astype(kind)


def bell_draw_with(rng, dims, scale, reach, shards, heavy, held_as=jnp.bfloat16):
    drawn = scale * jax.random.normal(rng, dims, jnp.float32)
    if shards:
        drawn = drawn * levels(rng, dims, shards, -0.22, 0.18)
    return jnp.clip(strengthened(drawn, jax.random.fold_in(rng, 3), *heavy), -reach, reach).astype(held_as)


def setup_inputs(seed: int = 0) -> dict:
    key_of = jax.random.split(jax.random.key(seed), 12)
    return {
        "block_input": normal_values(key_of[0], (TOKENS, D), 1.0, 6.0, ((0, 16),)),
        "segment_ids": jnp.searchsorted(jnp.cumsum(uneven(key_of[1], TOKENS * 5 // (4 * IMG), TOKENS, IMG, 0)), jnp.arange(TOKENS), side="right").astype(jnp.int32),
        "gain_one": jnp.clip(1.0 + 0.1 * jax.random.normal(key_of[2], (D,), jnp.float32), 0.5, 1.5),
        "shift_one": normal_values(key_of[3], (D,), 0.5, 3.0, (), jnp.float32),
        "qkv_weight": normal_values(key_of[4], (D, 3, D), D ** -0.5, 0.21875, ((2, 2),)),
        "out_weight": normal_values(key_of[5], (D, D), (D // 32) ** -0.5, 1.25, ((0, 2),)),
        "gain_two": jnp.clip(1.0 + 0.1 * jax.random.normal(key_of[6], (D,), jnp.float32), 0.5, 1.5),
        "shift_two": normal_values(key_of[7], (D,), 0.5, 3.0, (), jnp.float32),
        "up_weight": normal_values(key_of[8], (D, FF), D ** -0.5, 0.21875, ((1, 2),)),
        "down_weight": normal_values(key_of[9], (FF, D), FF ** -0.5, 0.109375, ((0, 2),)),
        "out_cotangent": bell_draw_with(key_of[10], (TOKENS, D), 1.0, 6.0, ((0, 16),), (0, 1, 16, 2.0)),
    }


EPSILON = 1e-05
MASKED = -1e+30

@jax.custom_vjp
def low(v):
    return lax.optimization_barrier(v.astype(jnp.bfloat16)).astype(jnp.float32)

@jax.custom_vjp
def low_back(v):
    return v

def low_keep(v):
    return (low(v), None)

def low_pass(kept, grad):
    return (grad,)

def back_keep(v):
    return (v, None)

def back_low(kept, grad):
    return (low(grad),)
low.defvjp(low_keep, low_pass)
low_back.defvjp(back_keep, back_low)

def layer_norm(values, gain, shift):
    centre = values - lax.optimization_barrier(jnp.mean(values, axis=-1, keepdims=True))
    spread = lax.optimization_barrier(jnp.mean(centre * centre, axis=-1, keepdims=True))
    return centre * lax.rsqrt(spread + EPSILON) * gain + shift

def attend_sequence(packed):
    query_rows, key_rows, value_rows, ids_row = packed
    scores = jnp.einsum('qhd,khd->hqk', query_rows, key_rows, precision=lax.Precision.HIGHEST) * HD ** (-0.5)
    scores = low_back(scores)
    same = ids_row[:, None] == ids_row[None, :]
    scores = jnp.where(same[None], scores, MASKED)
    top = lax.optimization_barrier(jnp.max(scores, axis=-1, keepdims=True))
    expo = jnp.exp(scores - top)
    probs = low(expo / lax.optimization_barrier(jnp.sum(expo, axis=-1, keepdims=True)))
    return jnp.einsum('hqk,khd->qhd', probs, value_rows, precision=lax.Precision.HIGHEST)

def forward(inputs, gain_a, shift_a, qkv_w, out_w, gain_b, shift_b, up_w, down_w, ids_group):
    rows = inputs.shape[0]
    normed_a = low(layer_norm(inputs, gain_a, shift_a))
    joint = jnp.einsum('td,dcf->tcf', normed_a, qkv_w, precision=lax.Precision.HIGHEST)
    joint = low(low_back(joint))
    shaped = joint.reshape(rows // SEQ, SEQ, 3, H, HD)
    mixed = lax.map(jax.checkpoint(attend_sequence), (shaped[:, :, 0], shaped[:, :, 1], shaped[:, :, 2], ids_group.reshape(rows // SEQ, SEQ)))
    mixed = low(low_back(mixed.reshape(rows, D)))
    branch_a = low_back(jnp.dot(mixed, out_w, precision=lax.Precision.HIGHEST))
    middle = inputs + branch_a
    normed_b = low(layer_norm(middle, gain_b, shift_b))
    hidden = low_back(jnp.dot(normed_b, up_w, precision=lax.Precision.HIGHEST))
    active = low(jax.nn.gelu(hidden, approximate=False))
    branch_b = low_back(jnp.dot(active, down_w, precision=lax.Precision.HIGHEST))
    return middle + branch_b

def reference(block_input, segment_ids, gain_one, shift_one, qkv_weight, out_weight, gain_two, shift_two, up_weight, down_weight, out_cotangent):
    number = TOKENS // SEQ
    group = 4 if number % 4 == 0 else 1
    rounds = number // group
    params = tuple((member.astype(jnp.float32) for member in (gain_one, shift_one, qkv_weight, out_weight, gain_two, shift_two, up_weight, down_weight)))
    inputs_all = block_input.astype(jnp.float32).reshape(rounds, group * SEQ, D)
    cotangent_all = out_cotangent.astype(jnp.float32).reshape(rounds, group * SEQ, D)
    ids_all = segment_ids.astype(jnp.int32).reshape(rounds, group * SEQ)

    def one_group(totals, packed):
        inputs, ids_group, cotangent = packed

        def tied(inputs_here, *weights):
            return forward(inputs_here, *weights, ids_group)
        result, pullback = jax.vjp(tied, inputs, *params)
        grads = pullback(cotangent)
        totals = tuple((first + second for first, second in zip(totals, grads[1:])))
        return (totals, (result.astype(jnp.bfloat16), grads[0].astype(jnp.bfloat16)))
    zeros = tuple((jnp.zeros_like(member) for member in params))
    totals, (outputs, input_grads) = lax.scan(one_group, zeros, (inputs_all, ids_all, cotangent_all))
    norm_grads = jnp.stack([totals[0], totals[1], totals[4], totals[5]])
    return (outputs.reshape(TOKENS, D), input_grads.reshape(TOKENS, D), totals[2], totals[3], totals[6], totals[7], norm_grads)
```

```python
import functools

import jax
import jax.numpy as jnp
import numpy as np
from jax import lax
from jax.experimental import pallas as pl
from jax.experimental.pallas import tpu as pltpu
from jax.sharding import PartitionSpec as P

HD = 48
SEQ = 1024
IMG = 256
MID = SEQ // 2
HALF_IMG = IMG // 2
WIN = MID + HALF_IMG
LOW = MID - HALF_IMG
EPSILON = 1e-05
MASKED = -1e30
F32 = jnp.float32
BF16 = jnp.bfloat16
SCALE = float(HD ** (-0.5))
SCALE2 = float(HD ** (-0.5) * np.log2(np.e))
HALF_LOG2E = float(0.5 * np.log2(np.e))
INV_SQRT_2PI = 0.3989422804014327
PHI = (
    0.11962326238213554,
    0.12084553903880502,
    0.09934703796123681,
    0.13041684726157698,
    -0.05716832560524514,
    0.21011968093231104,
    -0.1593792042147725,
    0.036195106181360036,
)
TILE = 512
UNROLL = 4
BANDS = ((0, 256, 0, 512), (256, 256, 0, 640), (512, 128, 256, 384))
VMEM_LIMIT = 63 << 20


def dot(a, b, ca, cb):
    return lax.dot_general(a, b, (((ca,), (cb,)), ((), ())), preferred_element_type=F32)


def standardize(values):
    centre = values - jnp.mean(values, axis=-1, keepdims=True)
    inverse = lax.rsqrt(jnp.mean(centre * centre, axis=-1, keepdims=True) + EPSILON)
    return centre * inverse, inverse


def norm_input_grad(xh, inverse, grad, gain):
    dhg = grad * gain
    return inverse * (
        dhg - jnp.mean(dhg, axis=-1, keepdims=True) - xh * jnp.mean(dhg * xh, axis=-1, keepdims=True)
    )


def normal_parts(u):
    t = 1.0 / (1.0 + 0.3 * jnp.abs(u))
    bell = jnp.exp2(u * u * (-HALF_LOG2E))
    poly = PHI[-1]
    for coefficient in PHI[-2::-1]:
        poly = poly * t + coefficient
    tail = poly * t * bell
    return jnp.where(u >= 0, 1.0 - tail, tail), bell * INV_SQRT_2PI


def half_index(index, bit):
    return (index // bit) % 2


class Links:
    def __init__(self, sems, dp, bits):
        self.sems, self.count, self.known = sems, 0, {}
        self.me, self.side = lax.axis_index("dp"), lax.axis_index("tp")
        self.bits = bits

    def semaphore(self, name, number=0, many=1):
        if name not in self.known:
            self.known[name] = self.count
            self.count += many
        return self.sems.at[self.known[name] + number]

    def partner(self, bit):
        if bit == 0:
            return {"tp": 1 - self.side}
        return {"dp": self.me + bit * (1 - 2 * half_index(self.me, bit))}

    def enter(self):
        barrier = pltpu.get_barrier_semaphore()
        for bit in self.bits:
            pl.semaphore_signal(barrier, inc=1, device_id=self.partner(bit), device_id_type=pl.DeviceIdType.MESH)
        pl.semaphore_wait(barrier, len(self.bits))

    def send(self, name, bit, src, dst, number=0, many=1):
        return pltpu.make_async_remote_copy(
            src_ref=src,
            dst_ref=dst,
            send_sem=self.semaphore(name + " out", number, many),
            recv_sem=self.semaphore(name + " in", number, many),
            device_id=self.partner(bit),
            device_id_type=pl.DeviceIdType.MESH,
        )

    def fetch(self, name, src, dst):
        return pltpu.make_async_copy(src, dst, self.semaphore(name))


SEMAPHORES = 256
UNITS = 7


def layer_kernel(
    dp,
    x_hbm, c_hbm, ids_ref, g1_ref, b1_ref, g2_ref, b2_ref, qkv_hbm, ow_hbm, up_hbm, dw_hbm,
    out_hbm, ig_hbm, qg_ref, pgt_ref, ug_ref, dgt_ref, ng_ref,
    sems, wq, wo, wu, wd, xw, cw, na, nat, jt, mixt, lses, bias, owned, nbt, ct, mid, acc, gacc, shared_in, shared_out,
    g_unit, rc, rx, rz1, rz2, ry, g_qkv, rq_c, rq_y, rq_x, rq_z1, rq_z2, norms,
):
    top = dp // 16
    core_bit, wide_bit = 1, 4
    c_bit, x_bit, z_bit, zz_bit = top, 2 * top, 4 * top, 8 * top
    bits = [0] + sorted({core_bit, wide_bit, c_bit, x_bit, z_bit, zz_bit})
    links = Links(sems, dp, bits)
    me, side = links.me, links.side
    width = xw.shape[1]
    heads_width = jt.shape[2]
    hidden = wu.shape[2]
    tiles = hidden // TILE
    heads = heads_width // HD
    first = pl.multiple_of(LOW * side, 128)
    at_c, at_x, at_z, at_zz = (half_index(me, bit) for bit in (c_bit, x_bit, z_bit, zz_bit))

    loads = {
        "x": links.fetch("x", x_hbm.at[pl.ds(first, WIN)], xw),
        "qkv": links.fetch("qkv", qkv_hbm, wq.at[0]),
        "c": links.fetch("c", c_hbm.at[pl.ds(first, WIN)], cw),
        "ow": links.fetch("ow", ow_hbm, wo.at[0]),
        "up": links.fetch("up", up_hbm, wu.at[0]),
        "dw": links.fetch("dw", dw_hbm, wd.at[0]),
    }
    for load in loads.values():
        load.start()

    quarter = 2 * half_index(me, wide_bit) + half_index(me, core_bit)
    quarter_wide = 2 * (1 - half_index(me, wide_bit)) + half_index(me, core_bit)
    chunks = [(qkv_hbm.at[j], wq.at[1, j]) for j in range(3)] + [(ow_hbm, wo.at[1])]
    for tile in range(tiles):
        cols = pl.ds(tile * TILE, TILE)
        chunks.append((up_hbm.at[:, cols], wu.at[1, :, cols]))
        chunks.append((dw_hbm.at[cols], wd.at[1, cols]))

    def piece(ref, index):
        size = ref.shape[0] // 4
        return ref.at[pl.ds(pl.multiple_of(index * size, 16), size)]

    def gather(step, n):
        src, dst = chunks[n]
        if step == "side":
            copy = (0, piece(src, quarter), piece(dst, quarter))
        elif step == "wide":
            copy = (wide_bit, piece(dst, quarter), piece(dst, quarter))
        elif step == "near":
            copy = (core_bit, piece(dst, quarter), piece(dst, quarter))
        else:
            copy = (core_bit, piece(dst, quarter_wide), piece(dst, quarter_wide))
        return links.send("gather " + step, *copy, number=n, many=len(chunks))

    def gather_first(numbers):
        for n in numbers:
            gather("side", n).start()

    def gather_second(numbers):
        for n in numbers:
            gather("side", n).wait()
            gather("wide", n).start()
            gather("near", n).start()

    def gather_third(numbers):
        for n in numbers:
            gather("wide", n).wait()
            gather("far", n).start()

    def gather_last(numbers):
        for n in numbers:
            gather("near", n).wait()
            gather("far", n).wait()

    links.enter()
    gather_first(range(4))

    ids = ids_ref[...]
    columns = ids.T
    row_ids = jnp.concatenate([ids[i : i + 1] for i in range(8)], axis=1)
    column_ids = jnp.concatenate([columns[:, i : i + 1] for i in range(8)], axis=0)
    low = side == 0
    row_ids = jnp.where(low, row_ids[:, :WIN], row_ids[:, LOW:])
    column_ids = jnp.where(low, column_ids[:WIN], column_ids[LOW:])
    bias[...] = jnp.where(column_ids == row_ids, 0.0, MASKED)
    middle_id = ids[MID // 128 : MID // 128 + 1, 0:1]
    begins = jnp.sum(jnp.where(ids < middle_id, 1.0, 0.0), axis=(0, 1), keepdims=True)
    ends = jnp.sum(jnp.where(ids <= middle_id, 1.0, 0.0), axis=(0, 1), keepdims=True)
    split = jnp.where(MID - begins <= ends - MID, begins, ends)
    sign = jnp.where(low, 1.0, -1.0)
    position = lax.broadcasted_iota(jnp.int32, (WIN, 1), 0).astype(F32) + (LOW * side).astype(F32)
    owned[...] = jnp.broadcast_to(jnp.where((position + 0.5 - split) * sign < 0, 1.0, 0.0), owned.shape)

    def row(ref):
        return ref[...].reshape(1, width)

    def project(half):
        for j in range(3):
            jt[half, j] = dot(wq[half, j], na[...], 0, 1).astype(BF16)

    def attend(half):
        @pl.loop(0, heads // UNROLL)
        def _(group):
            for u in range(UNROLL):
                head = group * UNROLL + u
                rows = pl.ds(pl.multiple_of(head * HD, 16), HD)
                out_rows = pl.ds(pl.multiple_of(half * heads_width + head * HD, 16), HD)
                q = jt[half, 0, rows, :]
                k = jt[half, 1, rows, :].T
                v = jt[half, 2, rows, :]
                v = jnp.concatenate([v, jnp.ones((16, WIN), BF16)], axis=0)
                for t0, tn, s0, sn in BANDS:
                    st = dot(k[s0 : s0 + sn], q[:, t0 : t0 + tn], 1, 0) * SCALE2 + bias[s0 : s0 + sn, t0 : t0 + tn]
                    most = jnp.max(st, axis=0, keepdims=True)
                    expo = jnp.exp2(st - most)
                    res = dot(expo.astype(BF16), v[:, s0 : s0 + sn], 0, 1).T
                    total = res[HD : HD + 1]
                    mixt[out_rows, t0 : t0 + tn] = (res[:HD] * (1.0 / total)).astype(BF16)
                    lses[half * heads + head, :, t0 : t0 + tn] = most + jnp.log2(total)

    loads["x"].wait()
    xh, unused = standardize(xw[...].astype(F32))
    na[...] = (xh * row(g1_ref) + row(b1_ref)).astype(BF16)
    nat[...] = na[...].T
    loads["qkv"].wait()
    project(0)
    gather_first((4, 5))
    attend(0)
    loads["c"].wait()
    cw[...] = (cw[...].astype(F32) * owned[...][:, 0:1]).astype(BF16)
    ct[...] = cw[...].T
    gather_second(range(4))
    gather_first((6, 7))
    gather_third(range(4))
    gather_last(range(3))
    project(1)
    attend(1)
    gather_second((4, 5))
    gather_first((8, 9))

    loads["ow"].wait()
    gather_last((3,))
    mid[...] = xw[...].astype(F32) + dot(mixt[0:heads_width], wo[0], 0, 0) + dot(mixt[heads_width:], wo[1], 0, 0)
    xh, unused = standardize(mid[...])
    na[...] = (xh * row(g2_ref) + row(b2_ref)).astype(BF16)
    nbt[...] = na[...].T
    acc[...] = mid[...]
    gacc[...] = jnp.zeros_like(gacc)
    loads["up"].wait()
    loads["dw"].wait()

    def unit_c(u):
        return links.send("unit c", c_bit, g_unit.at[u % 2, :, :, :, 1 - at_c], rc.at[u], number=u, many=UNITS)

    def unit_x(u):
        return links.send("unit x", x_bit, rc.at[u, :, :, 1 - at_x], rx.at[u], number=u, many=UNITS)

    def unit_z(u):
        return links.send("unit z", z_bit, rx.at[u, :, 1 - at_z], rz1.at[u], number=u, many=UNITS)

    def unit_zz(u):
        return links.send("unit zz", zz_bit, rz1.at[u, 1 - at_zz], rz2.at[u], number=u, many=UNITS)

    def unit_y(u):
        return links.send("unit y", 0, rz2.at[u], ry.at[u - tiles], number=u - tiles, many=tiles + 1)

    def plus(a, b):
        return a.astype(F32) + b.astype(F32)

    def stage_x(u):
        unit_c(u).wait()
        rc[u] = plus(rc[u], g_unit[u % 2, :, :, :, at_c]).astype(BF16)
        unit_x(u).start()

    def stage_z(u):
        unit_x(u).wait()
        rx[u] = plus(rx[u], rc[u, :, :, at_x]).astype(BF16)
        unit_z(u).start()

    def stage_zz(u):
        unit_z(u).wait()
        rz1[u] = plus(rz1[u], rx[u, :, at_z]).astype(BF16)
        unit_zz(u).start()

    def stage_y(u):
        unit_zz(u).wait()
        total = plus(rz2[u], rz1[u, at_zz])
        if u < tiles:
            ug_ref[:, u * TILE : (u + 1) * TILE] = total[:, :TILE]
            dgt_ref[:, u * TILE : (u + 1) * TILE] = total[:, TILE:]
        else:
            if u == 2 * tiles:
                pgt_ref[...] = total[:, :heads_width]
            rz2[u] = total.astype(BF16)
            unit_y(u).start()

    def stage_end(u):
        unit_y(u).wait()
        f = u - tiles
        if u < 2 * tiles:
            ug_ref[:, f * TILE : (f + 1) * TILE] += ry[f, :, :TILE].astype(F32)
            dgt_ref[:, f * TILE : (f + 1) * TILE] += ry[f, :, TILE:].astype(F32)
        else:
            pgt_ref[...] += ry[f, :, heads_width : 2 * heads_width].astype(F32)

    blocks = (2, 2, 2, 2, width // 16)

    @pl.loop(0, 2 * tiles)
    def _(u):
        half, tile = u // tiles, u % tiles
        cols = pl.ds(pl.multiple_of(tile * TILE, TILE), TILE)

        @pl.when(u == 1)
        def _():
            gather_third((4, 5))
            gather_second((6, 7))

        @pl.when(u == 3)
        def _():
            gather_last((4, 5))
            gather_third((6, 7))
            gather_second((8, 9))

        @pl.when(u == 4)
        def _():
            gather_last((6, 7))

        @pl.when(u == 5)
        def _():
            gather_third((8, 9))
            gather_last((8, 9))

        up = wu[half, :, cols]
        down = wd[half, cols, :]
        hid = dot(na[...], up, 1, 0)
        grad_active = dot(cw[...], down, 1, 1)
        phi_sum, phi = normal_parts(hid)
        active = (hid * phi_sum).astype(BF16)
        grad_hidden = (grad_active * (phi_sum + hid * phi)).astype(BF16)
        slot = u % 2
        g_unit[slot, :, :, :, :, :, TILE:] = dot(ct[...], active, 1, 0).astype(BF16).reshape(*blocks, TILE)
        g_unit[slot, :, :, :, :, :, :TILE] = dot(nbt[...], grad_hidden, 1, 0).astype(BF16).reshape(*blocks, TILE)
        unit_c(u).start()
        acc[...] += dot(active, down, 1, 0)
        gacc[...] += dot(grad_hidden, up, 1, 1)

        @pl.when(u >= 1)
        def _():
            stage_x(u - 1)

        @pl.when(u >= 4)
        def _():
            stage_z(u - 4)

    def exchange(name, hbm, slot):
        mine = na.at[pl.ds(pl.multiple_of((WIN - LOW) * side, 128), LOW)]
        rows = hbm.at[pl.ds(pl.multiple_of(WIN * side, 128), LOW)]
        common = pl.ds(pl.multiple_of(LOW * (1 - side), 128), WIN - LOW)
        copies = [
            links.send(name + " common", 0, na.at[common], shared_in.at[slot]),
            links.send(name + " rows", 0, mine, rows),
            links.fetch(name + " keep", mine, rows),
        ]
        store = links.fetch(name + " store", shared_out, hbm.at[pl.ds(LOW, WIN - LOW)])

        def start_common():
            copies[0].start()

        def start_rows():
            copies[1].start()
            copies[2].start()

        def merge():
            copies[0].wait()
            keep = owned[common, :][:, 0:1] > 0.5
            shared_out[...] = jnp.where(keep, na[common, :].astype(F32), shared_in[slot].astype(F32)).astype(BF16)
            store.start()

        def finish():
            copies[1].wait()
            copies[2].wait()
            store.wait()

        return start_common, start_rows, merge, finish

    out_common, out_rows, out_merge, out_finish = exchange("out", out_hbm, 0)
    na[...] = acc[...].astype(BF16)
    out_common()
    out_rows()

    xh, inverse = standardize(mid[...])
    grad = gacc[...]
    norms[0, 2:3, :] = jnp.sum(grad * xh, axis=0, keepdims=True)
    norms[0, 3:4, :] = jnp.sum(grad, axis=0, keepdims=True)
    mid[...] = cw[...].astype(F32) + norm_input_grad(xh, inverse, grad, row(g2_ref))
    cw[...] = mid[...].astype(BF16)
    for half in range(2):
        nbt[half * heads_width : (half + 1) * heads_width] = dot(wo[half], cw[...], 1, 1).astype(BF16)
    last = 2 * tiles
    ct[...] = cw[...].T
    for half in range(2):
        part = slice(half * heads_width, (half + 1) * heads_width)
        g_unit[last % 2, :, :, :, :, :, part] = dot(ct[...], mixt[part], 1, 1).astype(BF16).reshape(*blocks, heads_width)
    unit_c(last).start()
    stage_x(last - 1)

    def prob_at(u):
        return wd.at[u // 2, pl.ds((u % 2) * WIN, WIN), pl.ds(0, WIN)]

    def grad_at(u):
        return wu.at[u // 2, pl.ds(0, WIN), pl.ds((u % 2) * width, WIN)]

    def attend_back(half, group):
        for u in range(UNROLL):
            head = group * UNROLL + u
            rows = pl.ds(pl.multiple_of(head * HD, 16), HD)
            out_rows = pl.ds(pl.multiple_of(half * heads_width + head * HD, 16), HD)
            q = jt[half, 0, rows, :]
            k = jt[half, 1, rows, :]
            v = jt[half, 2, rows, :]
            do = nbt[out_rows, :]
            delta = jnp.sum(do.astype(F32) * mixt[out_rows, :].astype(F32), axis=0, keepdims=True)
            lse = lses[half * heads + head]
            probs, grads = prob_at(u), grad_at(u)
            st = dot(k.T, q, 1, 0) * SCALE2 + (bias[...] - lse)
            p = jnp.exp2(st)
            dp_ = dot(v.T, do, 1, 0)
            ds = (p * (dp_ - delta)).astype(BF16)
            probs[...] = p.astype(BF16)
            grads[...] = ds
            jt[half, 0, rows, :] = (dot(ds, k, 0, 1) * SCALE).astype(BF16).T
            jt[half, 2, rows, :] = dot(probs[...], do, 1, 1).astype(BF16).T
            jt[half, 1, rows, :] = (dot(grads[...], q, 1, 1) * SCALE).astype(BF16).T

    def weight_grad(half):
        for j in range(3):
            g_qkv[:, :, :, :, j] = dot(nat[...], jt[half, j], 1, 1).astype(BF16).reshape(*blocks, heads_width)

    def qkv_c(half):
        return links.send("qkv c", c_bit, g_qkv.at[:, :, :, 1 - at_c], rq_c.at[half], number=half, many=2)

    qkv_y = links.send("qkv y", 0, rq_c.at[1], rq_y)
    qkv_x = links.send("qkv x", x_bit, rq_c.at[0, :, :, 1 - at_x], rq_x)
    qkv_z = links.send("qkv z", z_bit, rq_x.at[:, 1 - at_z], rq_z1)
    qkv_zz = links.send("qkv zz", zz_bit, rq_z1.at[1 - at_zz], rq_z2)

    @pl.loop(0, heads // UNROLL)
    def _(group):
        attend_back(1, group)

        @pl.when(group == 0)
        def _():
            stage_z(2)
            stage_zz(0)
            stage_x(last)

    weight_grad(1)
    qkv_c(1).start()
    stage_z(3)
    stage_zz(1)
    stage_zz(2)
    stage_y(0)
    out_merge()
    qkv_c(1).wait()
    rq_c[1] = plus(rq_c[1], g_qkv[:, :, :, at_c]).astype(BF16)
    qkv_y.start()

    @pl.loop(0, heads // UNROLL)
    def _(group):
        attend_back(0, group)

        @pl.when(group == 0)
        def _():
            stage_z(4)
            stage_zz(3)
            stage_y(1)
            stage_y(2)

    out_finish()
    ig_common, ig_rows, ig_merge, ig_finish = exchange("ig", ig_hbm, 1)
    common_rows = pl.ds(pl.multiple_of(LOW * (1 - side), 128), WIN - LOW)
    single_rows = pl.ds(pl.multiple_of((WIN - LOW) * side, 128), LOW)

    def input_grad(rows):
        grad = None
        for half in range(2):
            for j in range(3):
                part = dot(jt[half, j, :, rows], wq[half, j], 0, 1)
                grad = part if grad is None else grad + part
        xh, inverse = standardize(xw[rows, :].astype(F32))
        na[rows, :] = (mid[rows, :] + norm_input_grad(xh, inverse, grad, row(g1_ref))).astype(BF16)
        return jnp.sum(grad * xh, axis=0, keepdims=True), jnp.sum(grad, axis=0, keepdims=True)

    def norm_copy(n):
        return links.send("norms", (0, c_bit, x_bit, z_bit, zz_bit)[n], norms.at[2 * n], norms.at[2 * n + 1], number=n, many=5)

    def norm_step(n):
        norm_copy(n).wait()
        norms[2 * n + 2] = norms[2 * n] + norms[2 * n + 1]
        if n < 4:
            norm_copy(n + 1).start()

    gain_one, shift_one = input_grad(common_rows)
    ig_common()
    weight_grad(0)
    qkv_c(0).start()
    gain_two, shift_two = input_grad(single_rows)
    norms[0, 0:1, :] = gain_one + gain_two
    norms[0, 1:2, :] = shift_one + shift_two
    norms[0, 4:8, :] = jnp.zeros((4, width), F32)
    norm_copy(0).start()
    ig_rows()
    qkv_c(0).wait()
    rq_c[0] = plus(rq_c[0], g_qkv[:, :, :, at_c]).astype(BF16)
    qkv_y.wait()
    rq_c[0] = plus(rq_c[0], rq_y[...]).astype(BF16)
    qkv_x.start()
    stage_z(5)
    stage_zz(4)
    stage_y(3)
    stage_z(last)
    stage_zz(5)
    stage_y(4)
    norm_step(0)
    stage_zz(last)
    stage_y(5)
    norm_step(1)
    stage_y(last)
    norm_step(2)
    stage_end(tiles)
    stage_end(tiles + 1)
    stage_end(tiles + 2)
    norm_step(3)
    stage_end(last)
    qkv_x.wait()
    rq_x[...] = plus(rq_x[...], rq_c[0, :, :, at_x]).astype(BF16)
    qkv_z.start()
    norm_step(4)
    ng_ref[...] = norms[10]
    ig_merge()
    qkv_z.wait()
    rq_z1[...] = plus(rq_z1[...], rq_x[:, at_z]).astype(BF16)
    qkv_zz.start()
    qkv_zz.wait()
    qg_ref[...] = plus(rq_z2[...], rq_z1[at_zz])
    ig_finish()


def collect_kernel(*refs):
    count = (len(refs) - 3) // 3
    sources, norms, targets = refs[:count], refs[count], refs[count + 1 : 2 * count + 1]
    target, held, sems = refs[2 * count + 1], refs[2 * count + 2 : 3 * count + 2], refs[-1]
    loads = [pltpu.make_async_copy(a, b, sems.at[0, n]) for n, (a, b) in enumerate(zip(sources, held))]
    stores = [pltpu.make_async_copy(a, b, sems.at[1, n]) for n, (a, b) in enumerate(zip(held, targets))]
    for load in loads:
        load.start()
    rows, share = target.shape
    width = norms.shape[1]
    place = lax.broadcasted_iota(jnp.int32, (width, share), 0) - share * lax.axis_index("dp")
    pick = jnp.where(place == lax.broadcasted_iota(jnp.int32, (width, share), 1), 1.0, 0.0)
    target[...] = lax.dot_general(
        norms[...], pick, (((1,), (0,)), ((), ())), precision=lax.Precision.HIGHEST, preferred_element_type=F32
    )[:rows]
    for load, store in zip(loads, stores):
        load.wait()
        store.start()
    for store in stores:
        store.wait()


def local(
    dp,
    block_input,
    segment_ids,
    gain_one,
    shift_one,
    qkv_weight,
    out_weight,
    gain_two,
    shift_two,
    up_weight,
    down_weight,
    out_cotangent,
):
    rows, width = block_input.shape
    heads_width, hidden = out_weight.shape[0], up_weight.shape[1]
    block, unit = width // 16, 2 * TILE
    S, V = jax.ShapeDtypeStruct, pltpu.VMEM
    place = pl.BlockSpec(memory_space=pltpu.VMEM)
    far = pl.BlockSpec(memory_space=pl.ANY)
    halves = [2, 2, 2, 2]
    out, ig, qg, pgt, ug, dgt, ng = pl.pallas_call(
        functools.partial(layer_kernel, dp),
        out_shape=(
            S((rows, width), BF16),
            S((rows, width), BF16),
            S((3, block, heads_width), F32),
            S((block, heads_width), F32),
            S((block, hidden), F32),
            S((block, hidden), F32),
            S((8, width), F32),
        ),
        in_specs=[far, far] + [place] * 5 + [far] * 4,
        out_specs=[far, far] + [place] * 5,
        scratch_shapes=[
            pltpu.SemaphoreType.DMA((SEMAPHORES,)),
            V((2, 3, width, heads_width), BF16),
            V((2, heads_width, width), BF16),
            V((2, width, hidden), BF16),
            V((2, hidden, width), BF16),
            V((WIN, width), BF16),
            V((WIN, width), BF16),
            V((WIN, width), BF16),
            V((width, WIN), BF16),
            V((2, 3, heads_width, WIN), BF16),
            V((width, WIN), BF16),
            V((width // HD, 1, WIN), F32),
            V((WIN, WIN), F32),
            V((WIN, 128), F32),
            V((width, WIN), BF16),
            V((width, WIN), BF16),
            V((WIN, width), F32),
            V((WIN, width), F32),
            V((WIN, width), F32),
            V((2, WIN - LOW, width), BF16),
            V((WIN - LOW, width), BF16),
            V((2, *halves, block, unit), BF16),
            V((UNITS, *halves[1:], block, unit), BF16),
            V((UNITS, *halves[2:], block, unit), BF16),
            V((UNITS, *halves[3:], block, unit), BF16),
            V((UNITS, block, unit), BF16),
            V((4, block, unit), BF16),
            V((*halves, 3, block, heads_width), BF16),
            V((2, *halves[1:], 3, block, heads_width), BF16),
            V((*halves[1:], 3, block, heads_width), BF16),
            V((*halves[2:], 3, block, heads_width), BF16),
            V((*halves[3:], 3, block, heads_width), BF16),
            V((3, block, heads_width), BF16),
            V((11, 8, width), F32),
        ],
        compiler_params=pltpu.CompilerParams(
            vmem_limit_bytes=VMEM_LIMIT, collective_id=0, has_side_effects=True
        ),
        name="layer",
    )(
        block_input,
        out_cotangent,
        segment_ids.reshape(8, 128),
        gain_one,
        shift_one,
        gain_two,
        shift_two,
        qkv_weight.transpose(1, 0, 2),
        out_weight,
        up_weight,
        down_weight,
    )
    rest = dp // 16
    if rest > 1:
        groups = [list(range(g * rest, (g + 1) * rest)) for g in range(16)]
        scatter = functools.partial(lax.psum_scatter, axis_name="dp", axis_index_groups=groups, tiled=True)
        qg = scatter(qg, scatter_dimension=1)
        pgt, ug, dgt = (scatter(part, scatter_dimension=0) for part in (pgt, ug, dgt))
        ng = lax.psum(ng, "dp", axis_index_groups=groups)
    share = width // dp
    far = pl.BlockSpec(memory_space=pl.ANY)
    near = pl.BlockSpec(memory_space=pltpu.VMEM)
    results = (out, ig, qg, pgt, ug, dgt)
    out, ig, qg, pgt, ug, dgt, ng = pl.pallas_call(
        collect_kernel,
        out_shape=tuple(S(a.shape, a.dtype) for a in results) + (S((4, share), F32),),
        in_specs=[far] * 6 + [near],
        out_specs=[far] * 6 + [near],
        scratch_shapes=[V(a.shape, a.dtype) for a in results] + [pltpu.SemaphoreType.DMA((2, 6))],
        name="collect",
    )(*results, ng)
    return out, ig, qg.transpose(1, 0, 2), pgt.T, ug, dgt.T, ng


def solution(mesh):
    in_specs = (
        P("dp", None),
        P("dp"),
        P(),
        P(),
        P(None, None, "tp"),
        P("tp", None),
        P(),
        P(),
        P(None, "tp"),
        P("tp", None),
        P("dp", None),
    )
    out_specs = (
        P("dp", None),
        P("dp", None),
        P("dp", None, "tp"),
        P("tp", "dp"),
        P("dp", "tp"),
        P("tp", "dp"),
        P(None, "dp"),
    )
    step = functools.partial(local, mesh.shape["dp"])
    return jax.shard_map(step, mesh=mesh, in_specs=in_specs, out_specs=out_specs, check_vma=False)
```

```python
import functools

import jax
import jax.numpy as jnp
import numpy as np
from jax import lax
from jax.experimental import pallas as pl
from jax.experimental.pallas import tpu as pltpu
from jax.sharding import PartitionSpec as P

HD = 48
SEQ = 1024
IMG = 256
MID = SEQ // 2
HALF_IMG = IMG // 2
WIN = MID + HALF_IMG
LOW = MID - HALF_IMG
EPSILON = 1e-05
MASKED = -1e30
F32 = jnp.float32
BF16 = jnp.bfloat16
SCALE = float(HD ** (-0.5))
SCALE2 = float(HD ** (-0.5) * np.log2(np.e))
HALF_LOG2E = float(0.5 * np.log2(np.e))
INV_SQRT_2PI = 0.3989422804014327
PHI = (
    0.11962326238213554,
    0.12084553903880502,
    0.09934703796123681,
    0.13041684726157698,
    -0.05716832560524514,
    0.21011968093231104,
    -0.1593792042147725,
    0.036195106181360036,
)
TILE = 512
UNROLL = 4
UNROLL_FORWARD = 2
BANDS = ((0, 256, 0, 512), (256, 256, 0, 768), (512, 256, 256, 768), (768, 256, 512, 512))
BANDS_BACK = ((0, 256, 0, 512), (256, 256, 0, 640), (512, 128, 256, 384))
VMEM_LIMIT = 63 << 20
SEMAPHORES = 320
X, Z, ZZ, Y = range(4)
AXES = (ZZ, Z, X)
SIDE, WIDE, DEEP, HALF, NEAR, UNIT, MERGE, NORM, WIDE_HALF, DEEP_HALF = range(10)
OUT, QK, VALUE, UP, DOWN = 0, 1, 2, 3, 6
OUT_BLOCKS, QKV_BLOCKS = 6, 8
FIRST = (OUT, UP, DOWN, UP + 1, DOWN + 1)
SECOND = (UP + 2, DOWN + 2, QK, VALUE)
LOADED, PROJECTED, PREPARED, MIXED, READY, OTHER = range(6)
FORWARD, NEED, FEED, SECOND_NORM, BACK, TAIL = 10, 20, 30, 40, 50, 60


def dot(a, b, ca, cb):
    return lax.dot_general(a, b, (((ca,), (cb,)), ((), ())), preferred_element_type=F32)


def standardize(values):
    centre = values - jnp.mean(values, axis=-1, keepdims=True)
    inverse = lax.rsqrt(jnp.mean(centre * centre, axis=-1, keepdims=True) + EPSILON)
    return centre * inverse, inverse


def norm_input_grad(xh, inverse, grad, gain):
    dhg = grad * gain
    return inverse * (
        dhg - jnp.mean(dhg, axis=-1, keepdims=True) - xh * jnp.mean(dhg * xh, axis=-1, keepdims=True)
    )


def normal_parts(u):
    t = 1.0 / (1.0 + 0.3 * jnp.abs(u))
    bell = jnp.exp2(u * u * (-HALF_LOG2E))
    poly = PHI[-1]
    for coefficient in PHI[-2::-1]:
        poly = poly * t + coefficient
    tail = poly * t * bell
    return jnp.where(u >= 0, 1.0 - tail, tail), bell * INV_SQRT_2PI
ORDERS = (
    (Y, Z, X, ZZ),
    (Z, Y, X, ZZ),
    (X, Z, Y, ZZ),
    (X, Z, ZZ, Y),
    (X, Y, Z, ZZ),
    (X, Z, ZZ, Y),
)
SEQUENCE = (0, 1, 2, 3)


def back_step(n):
    return 1 - n // 2, n % 2


PLAN = {
    LOADED: ((SIDE, OUT),),
    PROJECTED: ((SIDE, UP),),
    FORWARD: ((SIDE, DOWN), (WIDE, OUT), (DEEP, OUT), (SIDE, UP + 1), (WIDE, UP), (DEEP, UP), (SIDE, DOWN + 1)),
    FORWARD + 3: ((WIDE, DOWN), (DEEP, DOWN), (HALF, OUT)),
    PREPARED: ((WIDE, UP + 1), (DEEP, UP + 1)),
    NEED: ((NEAR, OUT),),
    MIXED: ((HALF, UP), (WIDE, DOWN + 1), (DEEP, DOWN + 1), (HALF, DOWN), (HALF, UP + 1)),
    READY: ((SIDE, UP + 2),),
    FEED + 0: ((HALF, DOWN + 1), (SIDE, DOWN + 2), (WIDE, UP + 2), (DEEP, UP + 2)),
    NEED + 1: ((NEAR, UP), (NEAR, DOWN)),
    FEED + 1: ((SIDE, QK), (UNIT, 0), (SIDE, VALUE), (WIDE, DOWN + 2), (DEEP, DOWN + 2)),
    FEED + 2: ((HALF, UP + 2), (UNIT, 1)),
    NEED + 3: ((NEAR, UP + 1), (NEAR, DOWN + 1)),
    FEED + 3: ((WIDE, QK), (DEEP, QK), (UNIT, 2), (WIDE, VALUE), (DEEP, VALUE), (HALF, DOWN + 2)),
    FEED + 4: ((UNIT, 3), (HALF, QK)),
    NEED + 5: ((NEAR, UP + 2), (NEAR, DOWN + 2)),
    FEED + 5: ((UNIT, 4),),
    SECOND_NORM: ((UNIT, 5),),
    SECOND_NORM + 1: ((UNIT, 2),),
    SECOND_NORM + 2: ((HALF, VALUE), (UNIT, OUT_BLOCKS), (UNIT, OUT_BLOCKS + 1), (UNIT, 0), (UNIT, 4)),
    OTHER: ((NEAR, QK), (NEAR, VALUE)),
    BACK + 0: ((UNIT, 3), (UNIT, 5), (UNIT, OUT_BLOCKS), (UNIT, 0)),
    BACK + 1: ((UNIT, QKV_BLOCKS), (UNIT, OUT_BLOCKS + 1), (UNIT, 4), (UNIT, 0)),
    BACK + 2: ((UNIT, 5), (UNIT, QKV_BLOCKS + 1), (UNIT, OUT_BLOCKS), (UNIT, OUT_BLOCKS + 1), (UNIT, QKV_BLOCKS)),
    BACK + 3: (
        (UNIT, 2), (UNIT, QKV_BLOCKS + 2), (UNIT, 0), (UNIT, OUT_BLOCKS), (UNIT, 4), (UNIT, OUT_BLOCKS + 1),
        (UNIT, QKV_BLOCKS + 1),
    ),
    TAIL + 2: (
        (UNIT, OUT_BLOCKS), (UNIT, 2), (UNIT, 4), (UNIT, QKV_BLOCKS + 3), (NORM, 0), (UNIT, QKV_BLOCKS + 1),
        (UNIT, QKV_BLOCKS + 2), (UNIT, QKV_BLOCKS + 2), (UNIT, 2), (MERGE, 1), (UNIT, QKV_BLOCKS + 1),
        (UNIT, QKV_BLOCKS + 3), (NORM, 0), (UNIT, QKV_BLOCKS + 2), (UNIT, QKV_BLOCKS + 3), (NORM, 0),
        (UNIT, QKV_BLOCKS + 2), (UNIT, QKV_BLOCKS + 3), (NORM, 0), (UNIT, QKV_BLOCKS + 3), (NORM, 0),
    ),
}


def half_index(index, bit):
    return (index // bit) % 2


class Links:
    def __init__(self, sems, bits):
        self.sems, self.count, self.known = sems, 0, {}
        self.me, self.side = lax.axis_index("dp"), lax.axis_index("tp")
        self.bits = bits

    def semaphore(self, name, number=0, many=1):
        if name not in self.known:
            self.known[name] = self.count
            self.count += many
        return self.sems.at[self.known[name] + number]

    def partner(self, bit):
        if bit == 0:
            return {"tp": 1 - self.side}
        return {"dp": self.me + bit * (1 - 2 * half_index(self.me, bit))}

    def greet(self):
        barrier = pltpu.get_barrier_semaphore()
        for bit in self.bits:
            pl.semaphore_signal(barrier, inc=1, device_id=self.partner(bit), device_id_type=pl.DeviceIdType.MESH)

    def meet(self):
        pl.semaphore_wait(pltpu.get_barrier_semaphore(), len(self.bits))

    def send(self, name, bit, src, dst, number=0, many=1):
        return pltpu.make_async_remote_copy(
            src_ref=src,
            dst_ref=dst,
            send_sem=self.semaphore((name, 0), number, many),
            recv_sem=self.semaphore((name, 1), number, many),
            device_id=self.partner(bit),
            device_id_type=pl.DeviceIdType.MESH,
        )

    def fetch(self, name, src, dst):
        return pltpu.make_async_copy(src, dst, self.semaphore(name))


class Chunk:
    def __init__(self, links, name, bits, source, target, lead):
        self.links, self.name, self.source, self.target, self.lead = links, name, source, target, lead
        self.core_bit, self.wide_bit, self.deep_bit = bits

    def copy(self, step):
        near, wide, deep = (half_index(self.links.me, b) for b in (self.core_bit, self.wide_bit, self.deep_bit))
        rows = self.target.shape[self.lead + 2]
        lower = (rows // 2 + 15) // 16 * 16
        ahead = (slice(None),) * self.lead
        mine = (*ahead, 2 * deep + wide, near)
        first, second = pl.ds(0, lower), pl.ds(lower, rows - lower)
        bit, where = {
            SIDE: (0, mine),
            WIDE: (self.wide_bit, mine),
            DEEP: (self.deep_bit, mine),
            WIDE_HALF: (self.wide_bit, (*ahead, 2 * (1 - deep) + wide, near, second)),
            DEEP_HALF: (self.deep_bit, (*ahead, 2 * deep + 1 - wide, near, first)),
            NEAR: (self.core_bit, (*ahead, slice(None), near)),
        }[step]
        source = self.source if step == SIDE else self.target
        return self.links.send((step, self.name), bit, source.at[where], self.target.at[where])

    def act(self, step):
        if step == SIDE:
            self.copy(SIDE).wait()
            self.copy(WIDE).start()
            self.copy(DEEP).start()
        elif step == WIDE:
            self.copy(WIDE).wait()
            self.copy(DEEP_HALF).start()
        elif step == DEEP:
            self.copy(DEEP).wait()
            self.copy(WIDE_HALF).start()
        elif step == HALF:
            self.copy(WIDE_HALF).wait()
            self.copy(DEEP_HALF).wait()
            self.copy(NEAR).start()
        else:
            self.copy(NEAR).wait()


class Block:
    def __init__(self, links, name, order, bits, held, arrival, first, kept, store):
        self.links, self.name, self.order, self.bits, self.held, self.arrival = links, name, order, bits, held, arrival
        self.first, self.kept, self.store = first, kept, store
        self.done, self.rank, self.meeting = -1, 0, None

    def axes(self, rank):
        return [axis for axis in self.order if axis != Y][:rank]

    def cut(self, axis, rank, other):
        left = [a for a in AXES if a not in self.axes(rank)]
        side = half_index(self.links.me, self.bits[axis])
        return (slice(None),) * left.index(axis) + (1 - side if other else side,)

    def copy(self, axis, rank):
        source = self.held[rank].at[self.cut(axis, rank, True)]
        return self.links.send((UNIT, self.name, axis), self.bits[axis], source, self.held[rank + 1])

    def act(self):
        axis = self.order[self.done] if self.done >= 0 else None
        last = self.done == 3
        if axis is None:
            self.first.wait()
            self.held[0][...] += self.kept()
        elif axis == Y:
            self.meeting.wait()
            here, there = self.held[self.rank], self.arrival
        else:
            self.copy(axis, self.rank).wait()
            here, there = self.held[self.rank + 1], self.held[self.rank].at[self.cut(axis, self.rank, False)]
            self.rank += 1
        if axis is not None:
            if last and self.store is not None:
                self.store(here[...].astype(F32) + there[...].astype(F32))
            else:
                here[...] += there[...]
        self.done += 1
        if self.done == 4:
            return
        axis = self.order[self.done]
        if axis != Y:
            self.copy(axis, self.rank).start()
        elif self.arrival is None:
            self.meeting.start()


def pair_up(links, name, keeps, gives):
    rank = keeps.order.index(Y)
    meeting = links.send((UNIT, name, Y), 0, gives.held[rank], keeps.arrival)
    keeps.meeting = gives.meeting = meeting


def arrival_shape(order):
    before = order[: order.index(Y)]
    return [2] * (3 - len(before))


def layer_kernel(
    dp,
    x_hbm, c_hbm, ids_hbm, g1_hbm, b1_hbm, g2_hbm, b2_hbm, qkv_hbm, ow_hbm, up_hbm, dw_hbm,
    out_hbm, ig_hbm, qg_ref, pgt_ref, ug_ref, dgt_ref, ng_ref,
    sems, wq, wo, wu, wd, g1, b1, g2, b2, ids_ref, xw, cw, na_full, nat, jt, mixt, lses, lse_full,
    bias, nbt, ct, gmt, mid, acc, gacc, shared_in, shared_out, norms, g_unit, g_out, g_qkv, *landings,
):
    top = dp // 16
    near_bits = (1, 2, 4)
    c_bit = top
    axis_bits = {X: 2 * top, Z: 4 * top, ZZ: 8 * top}
    links = Links(sems, [0] + sorted({*near_bits, c_bit, *axis_bits.values()}))
    links.greet()
    me, side = links.me, links.side
    rows_all, width = xw.shape
    heads_width = jt.shape[2]
    tiles = wd.shape[1]
    heads = heads_width // HD
    first = pl.multiple_of(LOW * side, 128)
    window = pl.ds(first, WIN)
    window_there = pl.ds(pl.multiple_of(LOW * (1 - side), 128), WIN)
    at_c = half_index(me, c_bit)

    feed_rows = pl.ds(pl.multiple_of(MID * side, 128), MID)
    feed_in_window = pl.ds(pl.multiple_of(HALF_IMG * side, 128), MID)

    small = ((ids_hbm, ids_ref), (g1_hbm, g1), (b1_hbm, b1), (g2_hbm, g2), (b2_hbm, b2))
    loads = {"x": links.fetch("x", x_hbm, xw)}
    for n, (source, target) in enumerate(small):
        loads[n] = links.fetch(n, source, target)
    for j in range(3):
        loads["q", j] = links.fetch(("q", j), qkv_hbm.at[j], wq.at[0, j])
    loads["c"] = links.fetch("c", c_hbm.at[feed_rows], cw)
    late = {"o": links.fetch("o", ow_hbm, wo.at[0])}
    for tile in range(tiles):
        cols = pl.ds(tile * TILE, TILE)
        late["u", tile] = links.fetch(("u", tile), up_hbm.at[:, :, :, cols], wu.at[0, :, :, :, cols])
        late["d", tile] = links.fetch(("d", tile), dw_hbm.at[tile], wd.at[0, tile])
    for load in loads.values():
        load.start()

    chunks = {
        OUT: Chunk(links, OUT, near_bits, ow_hbm, wo.at[1], 0),
        QK: Chunk(links, QK, near_bits, qkv_hbm.at[0:2], wq.at[1, 0:2], 1),
        VALUE: Chunk(links, VALUE, near_bits, qkv_hbm.at[2], wq.at[1, 2], 0),
    }
    for tile in range(tiles):
        cols = pl.ds(tile * TILE, TILE)
        name = UP + tile
        chunks[name] = Chunk(links, name, near_bits, up_hbm.at[:, :, :, cols], wu.at[1, :, :, :, cols], 0)
        name = DOWN + tile
        chunks[name] = Chunk(links, name, near_bits, dw_hbm.at[tile], wd.at[1, tile], 0)

    blocks = {}
    merges = [None, None]
    norm_count = [0]

    def run(point):
        for action, which in PLAN.get(point, ()):
            if action == UNIT:
                blocks[which].act()
            elif action == MERGE:
                merges[which]()
            elif action == NORM:
                norm_step()
            else:
                chunks[which].act(action)

    links.meet()
    for name in FIRST:
        chunks[name].copy(SIDE).start()

    for n in range(len(small)):
        loads[n].wait()
    ids = ids_ref[...]
    columns = ids.T
    row_ids = jnp.concatenate([ids[i : i + 1] for i in range(rows_all // 128)], axis=1)
    column_ids = jnp.concatenate([columns[:, i : i + 1] for i in range(rows_all // 128)], axis=0)
    low = side == 0
    middle_id = ids[MID // 128 : MID // 128 + 1, 0:1]
    begins = jnp.sum(jnp.where(ids < middle_id, 1.0, 0.0), axis=(0, 1), keepdims=True)
    ends = jnp.sum(jnp.where(ids <= middle_id, 1.0, 0.0), axis=(0, 1), keepdims=True)
    split = jnp.where(MID - begins <= ends - MID, begins, ends)
    sign = jnp.where(low, 1.0, -1.0)
    position = lax.broadcasted_iota(jnp.int32, (1, WIN), 1).astype(F32) + (LOW * side).astype(F32)
    owned_row = jnp.where((position + 0.5 - split) * sign < 0, 1.0, 0.0)

    half_tile = 2 * HALF_IMG
    biases = (
        (acc.at[0:MID, 0:half_tile],),
        (gacc.at[0:MID, 0:half_tile], gacc.at[0:half_tile, half_tile : 2 * half_tile]),
        (mid.at[0:MID, 0:half_tile], mid.at[0:half_tile, half_tile : 2 * half_tile]),
        (acc.at[0:MID, half_tile : 2 * half_tile],),
    )
    for parts, (t0, tn, s0, sn) in zip(biases, BANDS):
        for part in parts:
            s1 = s0 + part.shape[0]
            part[...] = jnp.where(column_ids[s0:s1] == row_ids[:, t0 : t0 + tn], 0.0, MASKED)
            s0 = s1

    def row(ref):
        return ref[...].reshape(1, width)

    def weight(ref):
        value = ref[...]
        return value.reshape(-1, value.shape[-1])

    def in_unit(index):
        return g_unit.at[index // 2, index % 2]

    def head_at(ref, head):
        return ref.at[head // 4, (head // 2) % 2, head % 2]

    pairs = heads // 2

    def mixed_copy(pair):
        here = in_unit(3).at[pair // 2, pair % 2, :, :, window_there]
        return links.send("m", 0, here, mixt.at[pl.ds(heads + 2 * pair, 2)], number=pair, many=pairs)

    lse_copy = links.send("l", 0, lse_full.at[:, :, window_there], lses.at[pl.ds(heads, heads)])

    def attend(head):
        q = head_at(in_unit(0), head)[...]
        k = head_at(in_unit(1), head)[...].T
        v = jnp.concatenate([head_at(in_unit(2), head)[...], jnp.ones((16, rows_all), BF16)], axis=0)
        for parts, (t0, tn, s0, sn) in zip(biases, BANDS):
            added = jnp.concatenate([part[...] for part in parts], axis=0)
            st = dot(k[s0 : s0 + sn], q[:, t0 : t0 + tn], 1, 0) * SCALE2 + added
            most = jnp.max(st, axis=0, keepdims=True)
            expo = jnp.exp2(st - most)
            res = dot(expo.astype(BF16), v[:, s0 : s0 + sn], 0, 1).T
            total = res[HD : HD + 1]
            head_at(in_unit(3), head)[:, t0 : t0 + tn] = (res[:HD] * (1.0 / total)).astype(BF16)
            lse_full[head, :, t0 : t0 + tn] = most + jnp.log2(total)

    loads["x"].wait()
    xh, unused = standardize(xw[...].astype(F32))
    na_full[...] = (xh * row(g1) + row(b1)).astype(BF16)
    for j in range(3):
        loads["q", j].wait()
    run(LOADED)
    for j in range(3):
        part = dot(weight(wq.at[0, j]), na_full[...], 0, 1).astype(BF16)
        in_unit(j)[...] = part.reshape(2, 2, 2, HD, rows_all)
    for load in late.values():
        load.start()
    run(PROJECTED)
    for head in range(heads // 2):
        attend(head)
    for pair in range(pairs // 2):
        mixed_copy(pair).start()
    run(FORWARD)

    @pl.loop(pairs // 2, pairs)
    def _(pair):
        attend(2 * pair)
        attend(2 * pair + 1)
        mixed_copy(pair).start()
        for number in range(pairs // 2, pairs):

            @pl.when(pair == number)
            def _():
                run(FORWARD + number)

    lse_copy.start()
    for name in SECOND:
        chunks[name].copy(SIDE).start()
    loads["c"].wait()
    ct[...] = cw[...].T
    nat[...] = na_full[window, :].T
    row_ids = jnp.where(low, row_ids[:, :WIN], row_ids[:, LOW:])
    column_ids = jnp.where(low, column_ids[:WIN], column_ids[LOW:])
    bias[...] = jnp.where(column_ids == row_ids, 0.0, MASKED)
    for j in range(3):
        jt[0, j] = in_unit(j)[:, :, :, :, window].reshape(heads_width, WIN)
    mixt[0:heads] = in_unit(3)[:, :, :, :, window].reshape(heads, HD, WIN)
    lses[0:heads] = lse_full[:, :, window]
    run(PREPARED)
    run(NEED)
    late["o"].wait()
    for pair in range(pairs):
        mixed_copy(pair).wait()
    lse_copy.wait()
    run(MIXED)

    def mixed_rows(half):
        return mixt[half * heads : (half + 1) * heads, :, feed_in_window].reshape(heads_width, MID)

    fed = na_full.at[0:MID]
    middle = mid.at[feed_in_window]
    branch = dot(mixed_rows(0), weight(wo.at[0]), 0, 0) + dot(mixed_rows(1), weight(wo.at[1]), 0, 0)
    acc[...] = xw[feed_rows, :].astype(F32) + branch
    middle[...] = acc[...]
    xh, unused = standardize(acc[...])
    fed[...] = (xh * row(g2) + row(b2)).astype(BF16)
    nbt[...] = fed[...].T
    gacc[...] = jnp.zeros_like(gacc)
    for key, load in late.items():
        if key != "o":
            load.wait()

    unit = g_unit.shape[-1]
    f0, landings = landings[0], list(landings[1:])
    grid = (2, 2, 2, 2, width // 16)

    def block(name, pair, keeps, first_copy, kept, store, held0=None):
        held = [held0] if held0 is not None else [landings.pop(0)]
        held += [landings.pop(0) for _ in range(3)]
        arrival = landings.pop(0) if keeps else None
        blocks[name] = Block(
            links, name, ORDERS[pair], axis_bits, held, arrival, first_copy, kept, store if keeps else None
        )

    def unit_copy(u):
        return links.send("g", c_bit, g_unit.at[u % 2, :, :, :, 1 - at_c], f0.at[u], number=u, many=2 * tiles)

    def unit_store(tile, total):
        cols = slice(tile * TILE, (tile + 1) * TILE)
        ug_ref[:, cols] = total[:, :TILE]
        dgt_ref[:, cols] = total[:, TILE:]

    def out_copy(half):
        return links.send("h", c_bit, g_out.at[half, :, :, :, 1 - at_c], blocks[OUT_BLOCKS + half].held[0], half, 2)

    def out_store(total):
        pgt_ref[...] = total

    columns_back = UNROLL * HD

    def qkv_copy(g):
        return links.send("k", c_bit, g_qkv.at[SEQUENCE.index(g) % 2, :, :, :, 1 - at_c], blocks[QKV_BLOCKS + g].held[0], g, 4)

    def qkv_store(group, total):
        for j in range(3):
            cols = slice(j * columns_back, (j + 1) * columns_back)
            qg_ref[j, :, group * columns_back : (group + 1) * columns_back] = total[:, cols]

    for u in range(2 * tiles):
        kept = functools.partial(lambda u: g_unit[u % 2, :, :, :, at_c], u)
        store = functools.partial(unit_store, u // 2)
        block(u, u // 2, u % 2 == 0, unit_copy(u), kept, store, f0.at[u])
    for half in range(2):
        kept = functools.partial(lambda half: g_out[half, :, :, :, at_c], half)
        block(OUT_BLOCKS + half, tiles, half == 0, None, kept, out_store)
        blocks[OUT_BLOCKS + half].first = out_copy(half)
    for g in range(4):
        kept = functools.partial(lambda slot: g_qkv[slot, :, :, :, at_c], SEQUENCE.index(g) % 2)
        block(QKV_BLOCKS + g, tiles + 1 + g % 2, g >= 2, None, kept, functools.partial(qkv_store, g % 2))
        blocks[QKV_BLOCKS + g].first = qkv_copy(g)
    for tile in range(tiles):
        pair_up(links, tile, blocks[2 * tile], blocks[2 * tile + 1])
    pair_up(links, tiles, blocks[OUT_BLOCKS], blocks[OUT_BLOCKS + 1])
    for g in range(2):
        pair_up(links, tiles + 1 + g, blocks[QKV_BLOCKS + g + 2], blocks[QKV_BLOCKS + g])

    run(READY)

    @pl.loop(0, 2 * tiles)
    def _(u):
        half, tile = u % 2, u // 2
        cols = pl.ds(pl.multiple_of(tile * TILE, TILE), TILE)
        for number in range(1, 2 * tiles, 2):

            @pl.when(u == number)
            def _():
                run(NEED + number)

        up = weight(wu.at[half, :, :, :, cols])
        down = weight(wd.at[half, tile])
        hid = dot(fed[...], up, 1, 0)
        grad_active = dot(cw[...], down, 1, 1)
        phi_sum, phi = normal_parts(hid)
        active = (hid * phi_sum).astype(BF16)
        grad_hidden = (grad_active * (phi_sum + hid * phi)).astype(BF16)
        slot = u % 2
        g_unit[slot, :, :, :, :, :, TILE:] = dot(ct[...], active, 1, 0).astype(BF16).reshape(*grid, TILE)
        g_unit[slot, :, :, :, :, :, :TILE] = dot(nbt[...], grad_hidden, 1, 0).astype(BF16).reshape(*grid, TILE)
        unit_copy(u).start()
        acc[...] += dot(active, down, 1, 0)
        gacc[...] += dot(grad_hidden, up, 1, 1)
        for number in range(2 * tiles):

            @pl.when(u == number)
            def _():
                run(FEED + number)

    fed[...] = acc[...].astype(BF16)
    xh, inverse = standardize(middle[...])
    grad = gacc[...]
    norms[0, 2:3, :] = jnp.sum(grad * xh, axis=0, keepdims=True)
    norms[0, 3:4, :] = jnp.sum(grad, axis=0, keepdims=True)
    middle[...] = cw[...].astype(F32) + norm_input_grad(xh, inverse, grad, row(g2))
    cw[...] = middle[...].astype(BF16)
    edge_here = pl.ds(pl.multiple_of((MID - HALF_IMG) - 2 * HALF_IMG * side, 128), HALF_IMG)
    edge_there = pl.ds(pl.multiple_of(MID * side, 128), HALF_IMG)
    other_edge = pl.ds(pl.multiple_of(MID * (1 - side), 128), HALF_IMG)
    for half in range(2):
        part = slice(half * heads_width, (half + 1) * heads_width)
        gmt[part, feed_in_window] = dot(weight(wo.at[half]), cw[...], 1, 1).astype(BF16)
    edge_copies = []
    for half in range(2):
        here, there = (pl.ds(n * heads_width, heads_width) for n in (half, 1 - half))
        edge_copies.append(links.send("e", 0, gmt.at[here, edge_here], gmt.at[there, edge_there], number=half, many=2))
    out_copies = [
        links.send("r", 0, fed, out_hbm.at[feed_rows]),
        links.fetch("s", fed, out_hbm.at[feed_rows]),
    ]
    for copy in edge_copies + out_copies:
        copy.start()
    run(SECOND_NORM)
    ct[...] = cw[...].T
    for half in range(2):
        g_out[half] = dot(ct[...], mixed_rows(half), 1, 1).astype(BF16).reshape(*grid, heads_width)
        out_copy(half).start()
    run(SECOND_NORM + 1)
    for copy in edge_copies:
        copy.wait()
    gmt[...] = (gmt[...].astype(F32) * owned_row).astype(BF16)
    mid[other_edge, :] = jnp.zeros((HALF_IMG, width), F32)
    run(SECOND_NORM + 2)

    def attend_back(half, group):
        for u in range(UNROLL):
            head = group * UNROLL + u
            rows = pl.ds(pl.multiple_of(head * HD, 16), HD)
            out_rows = pl.ds(pl.multiple_of(half * heads_width + head * HD, 16), HD)
            q = jt[half, 0, rows, :]
            k = jt[half, 1, rows, :]
            v = jt[half, 2, rows, :]
            do = gmt[out_rows, :]
            mixed = mixt[half * heads + head]
            delta = jnp.sum(do.astype(F32) * mixed.astype(F32), axis=0, keepdims=True)
            lse = lses[half * heads + head]
            kt, vt = k.T, v.T
            grads = []
            for s0, sn, t0, tn in BANDS_BACK:
                ss, ts = slice(s0, s0 + sn), slice(t0, t0 + tn)
                st = dot(kt[ss], q[:, ts], 1, 0) * SCALE2 + (bias[ss, ts] - lse[:, ts])
                p = jnp.exp2(st)
                dprobs = dot(vt[ss], do[:, ts], 1, 0)
                ds = (p * (dprobs - delta[:, ts])).astype(BF16)
                grads.append(ds)
                jt[half, 2, rows, ss] = dot(p.astype(BF16), do[:, ts], 1, 1).astype(BF16).T
                jt[half, 1, rows, ss] = (dot(ds, q[:, ts], 1, 1) * SCALE).astype(BF16).T
            for q0, qn, unused, unused in BANDS_BACK:
                total = None
                for ds, (s0, sn, t0, tn) in zip(grads, BANDS_BACK):
                    if t0 <= q0 and q0 + qn <= t0 + tn:
                        part = dot(ds[:, q0 - t0 : q0 - t0 + qn], k[:, s0 : s0 + sn], 0, 1)
                        total = part if total is None else total + part
                jt[half, 0, rows, q0 : q0 + qn] = (total * SCALE).astype(BF16).T

    def weight_grad(n):
        half, group = back_step(n)
        rows = pl.ds(pl.multiple_of(group * columns_back, 16), columns_back)
        grads = jnp.concatenate([jt[half, j, rows, :] for j in range(3)], axis=0)
        g_qkv[n % 2] = dot(nat[...], grads, 1, 1).astype(BF16).reshape(*grid, 3 * columns_back)

    first_other = min(SEQUENCE.index(0), SEQUENCE.index(1))

    @pl.loop(0, 4)
    def _(n):
        @pl.when(n == first_other)
        def _():
            run(OTHER)
            for j in range(3):
                jt[1, j] = dot(weight(wq.at[1, j]), nat[...], 0, 0).astype(BF16)

        attend_back(*back_step(n))

        @pl.when(n < 3)
        def _():
            weight_grad(n)

        for number in range(4):

            @pl.when(n == number)
            def _():
                if number < 3:
                    qkv_copy(SEQUENCE[number]).start()
                run(BACK + number)

    for copy in out_copies:
        copy.wait()
    na = na_full.at[0:WIN]
    common_rows = pl.multiple_of(LOW * (1 - side), 128), WIN - LOW
    single_rows = pl.multiple_of((WIN - LOW) * side, 128), LOW
    common, single = pl.ds(*common_rows), pl.ds(*single_rows)
    single_there = pl.ds(pl.multiple_of(WIN * side, 128), LOW)
    ig_common = links.send("i", 0, na.at[common], shared_in)
    ig_copies = [
        links.send("j", 0, na.at[single], ig_hbm.at[single_there]),
        links.fetch("t", na.at[single], ig_hbm.at[single_there]),
        links.fetch("v", shared_out, ig_hbm.at[pl.ds(LOW, WIN - LOW)]),
    ]

    def merge():
        ig_common.wait()
        shared_out[...] = na[common, :] + shared_in[...]
        ig_copies[2].start()

    merges[1] = merge

    def input_grad(start, count):
        rows = pl.ds(start, count)
        grad = None
        for half in range(2):
            for j in range(3):
                part = dot(jt[half, j, :, rows], weight(wq.at[half, j]), 0, 1)
                grad = part if grad is None else grad + part
        xh, inverse = standardize(xw[pl.ds(pl.multiple_of(first + start, 128), count), :].astype(F32))
        na[rows, :] = (mid[rows, :] + norm_input_grad(xh, inverse, grad, row(g1))).astype(BF16)
        return jnp.sum(grad * xh, axis=0, keepdims=True), jnp.sum(grad, axis=0, keepdims=True)

    norm_bits = (c_bit, *axis_bits.values(), 0)

    def norm_copy(n):
        return links.send("w", norm_bits[n], norms.at[2 * n], norms.at[2 * n + 1], number=n, many=5)

    def norm_step():
        n = norm_count[0]
        norm_count[0] += 1
        norm_copy(n).wait()
        norms[2 * n + 2] = norms[2 * n] + norms[2 * n + 1]
        if n < 4:
            norm_copy(n + 1).start()

    gain_one, shift_one = input_grad(*common_rows)
    ig_common.start()
    run(TAIL)
    weight_grad(3)
    qkv_copy(SEQUENCE[3]).start()
    run(TAIL + 1)
    gain_two, shift_two = input_grad(*single_rows)
    for copy in ig_copies[:2]:
        copy.start()
    norms[0, 0:1, :] = gain_one + gain_two
    norms[0, 1:2, :] = shift_one + shift_two
    norms[0, 4:8, :] = jnp.zeros((4, width), F32)
    norm_copy(0).start()
    run(TAIL + 2)
    ng_ref[...] = norms[10]
    for copy in ig_copies:
        copy.wait()


def collect_kernel(*refs):
    count = (len(refs) - 3) // 3
    sources, norms, targets = refs[:count], refs[count], refs[count + 1 : 2 * count + 1]
    target, held, sems = refs[2 * count + 1], refs[2 * count + 2 : 3 * count + 2], refs[-1]
    loads = [pltpu.make_async_copy(a, b, sems.at[0, n]) for n, (a, b) in enumerate(zip(sources, held))]
    stores = [pltpu.make_async_copy(a, b, sems.at[1, n]) for n, (a, b) in enumerate(zip(held, targets))]
    for load in loads:
        load.start()
    rows, share = target.shape
    width = norms.shape[1]
    place = lax.broadcasted_iota(jnp.int32, (width, share), 0) - share * lax.axis_index("dp")
    pick = jnp.where(place == lax.broadcasted_iota(jnp.int32, (width, share), 1), 1.0, 0.0)
    target[...] = lax.dot_general(
        norms[...], pick, (((1,), (0,)), ((), ())), precision=lax.Precision.HIGHEST, preferred_element_type=F32
    )[:rows]
    for load, store in zip(loads, stores):
        load.wait()
        store.start()
    for store in stores:
        store.wait()


def local(
    dp,
    block_input,
    segment_ids,
    gain_one,
    shift_one,
    qkv_weight,
    out_weight,
    gain_two,
    shift_two,
    up_weight,
    down_weight,
    out_cotangent,
):
    rows, width = block_input.shape
    heads_width, hidden = out_weight.shape[0], up_weight.shape[1]
    block, unit, group, tiles = width // 16, 2 * TILE, 3 * UNROLL * HD, hidden // TILE
    heads = heads_width // HD
    S, V = jax.ShapeDtypeStruct, pltpu.VMEM
    place = pl.BlockSpec(memory_space=pltpu.VMEM)
    far = pl.BlockSpec(memory_space=pl.ANY)
    halves = [2, 2, 2, 2]
    landings = [V((2 * tiles, *halves[1:], block, unit), BF16)]
    kinds = [(u // 2, u % 2 == 0, unit, False) for u in range(2 * tiles)]
    kinds += [(tiles, half == 0, heads_width, True) for half in range(2)]
    kinds += [(tiles + 1 + g % 2, g >= 2, group, True) for g in range(4)]
    for pair, keeps, wide, whole in kinds:
        landings += [V((*halves[n:], block, wide), BF16) for n in range(1 if whole else 2, 5)]
        if keeps:
            landings.append(V((*arrival_shape(ORDERS[pair]), block, wide), BF16))
    out, ig, qg, pgt, ug, dgt, ng = pl.pallas_call(
        functools.partial(layer_kernel, dp),
        out_shape=(
            S((rows, width), BF16),
            S((rows, width), BF16),
            S((3, block, heads_width), F32),
            S((block, heads_width), F32),
            S((block, hidden), F32),
            S((block, hidden), F32),
            S((8, width), F32),
        ),
        in_specs=[far] * 11,
        out_specs=[far, far] + [place] * 5,
        scratch_shapes=[
            pltpu.SemaphoreType.DMA((SEMAPHORES,)),
            V((2, 3, 4, 2, width // 8, heads_width), BF16),
            V((2, 4, 2, heads_width // 8, width), BF16),
            V((2, 4, 2, width // 8, hidden), BF16),
            V((2, tiles, 4, 2, TILE // 8, width), BF16),
            *[V((width,), F32)] * 4,
            V((rows // 128, 128), jnp.int32),
            V((rows, width), BF16),
            V((MID, width), BF16),
            V((rows, width), BF16),
            V((width, WIN), BF16),
            V((2, 3, heads_width, WIN), BF16),
            V((2 * heads, HD, WIN), BF16),
            V((2 * heads, 1, WIN), F32),
            V((heads, 1, rows), F32),
            V((WIN, WIN), F32),
            V((width, MID), BF16),
            V((width, MID), BF16),
            V((width, WIN), BF16),
            V((WIN, width), F32),
            V((MID, width), F32),
            V((MID, width), F32),
            V((WIN - LOW, width), BF16),
            V((WIN - LOW, width), BF16),
            V((11, 8, width), F32),
            V((2, *halves, block, unit), BF16),
            V((2, *halves, block, heads_width), BF16),
            V((2, *halves, block, group), BF16),
            *landings,
        ],
        compiler_params=pltpu.CompilerParams(
            vmem_limit_bytes=VMEM_LIMIT, collective_id=0, has_side_effects=True
        ),
        name="layer",
    )(
        block_input,
        out_cotangent,
        segment_ids.reshape(rows // 128, 128),
        gain_one,
        shift_one,
        gain_two,
        shift_two,
        qkv_weight.transpose(1, 0, 2).reshape(3, 4, 2, width // 8, heads_width),
        out_weight.reshape(4, 2, heads_width // 8, width),
        up_weight.reshape(4, 2, width // 8, hidden),
        down_weight.reshape(tiles, 4, 2, TILE // 8, width),
    )
    rest = dp // 16
    if rest > 1:
        groups = [list(range(g * rest, (g + 1) * rest)) for g in range(16)]
        scatter = functools.partial(lax.psum_scatter, axis_name="dp", axis_index_groups=groups, tiled=True)
        qg = scatter(qg, scatter_dimension=1)
        pgt, ug, dgt = (scatter(part, scatter_dimension=0) for part in (pgt, ug, dgt))
        ng = lax.psum(ng, "dp", axis_index_groups=groups)
    share = width // dp
    results = (out, ig, qg, pgt, ug, dgt)
    out, ig, qg, pgt, ug, dgt, ng = pl.pallas_call(
        collect_kernel,
        out_shape=tuple(S(a.shape, a.dtype) for a in results) + (S((4, share), F32),),
        in_specs=[far] * 6 + [place],
        out_specs=[far] * 6 + [place],
        scratch_shapes=[V(a.shape, a.dtype) for a in results] + [pltpu.SemaphoreType.DMA((2, 6))],
        name="collect",
    )(*results, ng)
    return out, ig, qg.transpose(1, 0, 2), pgt.T, ug, dgt.T, ng


def solution(mesh):
    in_specs = (
        P("dp", None),
        P("dp"),
        P(),
        P(),
        P(None, None, "tp"),
        P("tp", None),
        P(),
        P(),
        P(None, "tp"),
        P("tp", None),
        P("dp", None),
    )
    out_specs = (
        P("dp", None),
        P("dp", None),
        P("dp", None, "tp"),
        P("tp", "dp"),
        P("dp", "tp"),
        P("tp", "dp"),
        P(None, "dp"),
    )
    step = functools.partial(local, mesh.shape["dp"])
    return jax.shard_map(step, mesh=mesh, in_specs=in_specs, out_specs=out_specs, check_vma=False)
```

```python
import functools

import jax
import jax.numpy as jnp
import numpy as np
from jax import lax
from jax.experimental import pallas as pl
from jax.experimental.pallas import tpu as pltpu
from jax.sharding import PartitionSpec as P

HD = 48
SEQ = 1024
IMG = 256
MID = SEQ // 2
HALF_IMG = IMG // 2
WIN = MID + HALF_IMG
LOW = MID - HALF_IMG
EPSILON = 1e-05
MASKED = -1e30
F32 = jnp.float32
BF16 = jnp.bfloat16
SCALE = float(HD ** (-0.5))
SCALE2 = float(HD ** (-0.5) * np.log2(np.e))
HALF_LOG2E = float(0.5 * np.log2(np.e))
INV_SQRT_2PI = 0.3989422804014327
PHI = (
    0.11962326238213554,
    0.12084553903880502,
    0.09934703796123681,
    0.13041684726157698,
    -0.05716832560524514,
    0.21011968093231104,
    -0.1593792042147725,
    0.036195106181360036,
)
TILE = 512
UNROLL = 4
UNROLL_FORWARD = 2
BANDS = ((0, 256, 0, 512), (256, 256, 0, 768), (512, 256, 256, 768), (768, 256, 512, 512))
BANDS_BACK = ((0, 256, 0, 512), (256, 256, 0, 640), (512, 128, 256, 384))
VMEM_LIMIT = 63 << 20
SEMAPHORES = 320
X, Z, ZZ, Y = range(4)
AXES = (ZZ, Z, X)
SIDE, WIDE, DEEP, CROSS, NEAR, UNIT, MERGE, NORM = range(8)
OUT, QKV, UP, DOWN = 0, 1, 2, 5
OUT_BLOCKS, QKV_BLOCKS = 6, 8
FIRST = (OUT, UP, DOWN, UP + 1, DOWN + 1)
SECOND = (UP + 2, DOWN + 2, QKV)
NEAR_BITS = (1, 4, 2)
LOADED, PROJECTED, PREPARED, MIXED, READY, OTHER = range(6)
FORWARD, NEED, MIDWAY, FEED, SECOND_NORM, BACK, TAIL = 10, 20, 30, 40, 50, 60, 70


def dot(a, b, ca, cb):
    return lax.dot_general(a, b, (((ca,), (cb,)), ((), ())), preferred_element_type=F32)


def standardize(values):
    centre = values - jnp.mean(values, axis=-1, keepdims=True)
    inverse = lax.rsqrt(jnp.mean(centre * centre, axis=-1, keepdims=True) + EPSILON)
    return centre * inverse, inverse


def norm_input_grad(xh, inverse, grad, gain):
    dhg = grad * gain
    return inverse * (
        dhg - jnp.mean(dhg, axis=-1, keepdims=True) - xh * jnp.mean(dhg * xh, axis=-1, keepdims=True)
    )


def normal_parts(u):
    t = 1.0 / (1.0 + 0.3 * jnp.abs(u))
    bell = jnp.exp2(u * u * (-HALF_LOG2E))
    poly = PHI[-1]
    for coefficient in PHI[-2::-1]:
        poly = poly * t + coefficient
    tail = poly * t * bell
    return jnp.where(u >= 0, 1.0 - tail, tail), bell * INV_SQRT_2PI
ORDERS = (
    (Y, Z, X, ZZ),
    (X, Z, Y, ZZ),
    (Z, X, Y, ZZ),
    (X, ZZ, Z, Y),
    (X, Y, Z, ZZ),
    (X, Y, Z, ZZ),
)
SEQUENCE = (0, 1, 2, 3)


def back_step(n):
    return 1 - n // 2, n % 2


PLAN = {
    LOADED: ((SIDE, OUT),),
    PROJECTED: ((SIDE, UP), (SIDE, DOWN), (DEEP, OUT)),
    FORWARD: ((SIDE, UP + 1), (DEEP, UP), (SIDE, DOWN + 1)),
    FORWARD + 2: ((DEEP, DOWN), (CROSS, OUT)),
    FORWARD + 3: ((DEEP, UP + 1),),
    PREPARED: ((DEEP, DOWN + 1), (CROSS, UP)),
    NEED + 9: ((NEAR, OUT),),
    READY: ((CROSS, DOWN),),
    MIDWAY + 0: ((SIDE, UP + 2),),
    FEED + 0: ((CROSS, UP + 1), (SIDE, DOWN + 2), (CROSS, DOWN + 1)),
    NEED + 1: ((NEAR, UP), (NEAR, DOWN)),
    MIDWAY + 1: ((DEEP, UP + 2),),
    FEED + 1: ((UNIT, 0), (DEEP, DOWN + 2), (SIDE, QKV)),
    NEED + 2: ((NEAR, UP + 1), (NEAR, DOWN + 1)),
    FEED + 2: ((UNIT, 1), (CROSS, UP + 2)),
    MIDWAY + 3: ((CROSS, DOWN + 2),),
    FEED + 3: ((UNIT, 2), (DEEP, QKV)),
    NEED + 4: ((NEAR, UP + 2), (NEAR, DOWN + 2)),
    FEED + 4: ((UNIT, 3),),
    FEED + 5: ((UNIT, 4), (CROSS, QKV)),
    SECOND_NORM: ((UNIT, 5), (UNIT, 2)),
    SECOND_NORM + 2: ((UNIT, OUT_BLOCKS), (UNIT, 0), (UNIT, OUT_BLOCKS + 1), (UNIT, 4), (UNIT, 3)),
    OTHER: ((NEAR, QKV),),
    BACK + 0: ((UNIT, OUT_BLOCKS), (UNIT, 5), (UNIT, OUT_BLOCKS + 1)),
    BACK + 1: ((UNIT, 2), (UNIT, QKV_BLOCKS), (UNIT, 4)),
    BACK + 2: ((UNIT, 5), (UNIT, QKV_BLOCKS + 1), (UNIT, 0), (UNIT, QKV_BLOCKS)),
    BACK + 3: ((UNIT, 3), (UNIT, 3), (UNIT, QKV_BLOCKS + 2), (UNIT, 5), (UNIT, OUT_BLOCKS), (UNIT, QKV_BLOCKS + 1)),
    TAIL: ((UNIT, OUT_BLOCKS + 1), (UNIT, QKV_BLOCKS + 3)),
    TAIL + 1: ((UNIT, 0), (UNIT, 3)),
    TAIL + 2: (
        (NORM, 0), (UNIT, QKV_BLOCKS + 2), (UNIT, QKV_BLOCKS + 2), (UNIT, 5), (UNIT, OUT_BLOCKS),
        (UNIT, OUT_BLOCKS + 1), (UNIT, QKV_BLOCKS + 3), (UNIT, QKV_BLOCKS + 3), (NORM, 0), (MERGE, 1), (UNIT, 0),
        (UNIT, QKV_BLOCKS + 2), (UNIT, QKV_BLOCKS + 3), (NORM, 0), (UNIT, QKV_BLOCKS + 2), (UNIT, QKV_BLOCKS + 3),
        (NORM, 0), (UNIT, OUT_BLOCKS), (NORM, 0),
    ),
}


def feed_half(u):
    return (u + u // 2 - u // 4) % 2


def half_index(index, bit):
    return (index // bit) % 2


class Links:
    def __init__(self, sems, bits):
        self.sems, self.count, self.known = sems, 0, {}
        self.me, self.side = lax.axis_index("dp"), lax.axis_index("tp")
        self.bits = bits

    def semaphore(self, name, number=0, many=1):
        if name not in self.known:
            self.known[name] = self.count
            self.count += many
        return self.sems.at[self.known[name] + number]

    def partner(self, bit):
        if bit == 0:
            return {"tp": 1 - self.side}
        return {"dp": self.me + bit * (1 - 2 * half_index(self.me, bit))}

    def greet(self):
        barrier = pltpu.get_barrier_semaphore()
        for bit in self.bits:
            pl.semaphore_signal(barrier, inc=1, device_id=self.partner(bit), device_id_type=pl.DeviceIdType.MESH)

    def meet(self):
        pl.semaphore_wait(pltpu.get_barrier_semaphore(), len(self.bits))

    def send(self, name, bit, src, dst, number=0, many=1):
        return pltpu.make_async_remote_copy(
            src_ref=src,
            dst_ref=dst,
            send_sem=self.semaphore((name, 0), number, many),
            recv_sem=self.semaphore((name, 1), number, many),
            device_id=self.partner(bit),
            device_id_type=pl.DeviceIdType.MESH,
        )

    def fetch(self, name, src, dst):
        return pltpu.make_async_copy(src, dst, self.semaphore(name))


class Chunk:
    def __init__(self, links, name, bits, source, target, lead):
        self.links, self.name, self.source, self.target, self.lead = links, name, source, target, lead
        self.core_bit, self.wide_bit, self.deep_bit = bits

    def copy(self, step):
        near, wide, deep = (half_index(self.links.me, b) for b in (self.core_bit, self.wide_bit, self.deep_bit))
        ahead = (slice(None),) * self.lead
        mine = (*ahead, 2 * deep + wide, near)
        bit, where = {
            SIDE: (0, mine),
            WIDE: (self.wide_bit, mine),
            DEEP: (self.deep_bit, mine),
            CROSS: (self.wide_bit, (*ahead, 2 * (1 - deep) + wide, near)),
            NEAR: (self.core_bit, (*ahead, slice(None), near)),
        }[step]
        source = self.source if step == SIDE else self.target
        return self.links.send((step, self.name), bit, source.at[where], self.target.at[where])

    def act(self, step):
        if step == SIDE:
            self.copy(SIDE).wait()
            self.copy(WIDE).start()
            self.copy(DEEP).start()
        elif step == DEEP:
            self.copy(DEEP).wait()
            self.copy(CROSS).start()
        elif step == CROSS:
            self.copy(WIDE).wait()
            self.copy(CROSS).wait()
            self.copy(NEAR).start()
        else:
            self.copy(NEAR).wait()


class Block:
    def __init__(self, links, name, order, bits, held, arrival, first, kept, store):
        self.links, self.name, self.order, self.bits, self.held, self.arrival = links, name, order, bits, held, arrival
        self.first, self.kept, self.store = first, kept, store
        self.done, self.rank, self.meeting = -1, 0, None

    def axes(self, rank):
        return [axis for axis in self.order if axis != Y][:rank]

    def cut(self, axis, rank, other):
        left = [a for a in AXES if a not in self.axes(rank)]
        side = half_index(self.links.me, self.bits[axis])
        return (slice(None),) * left.index(axis) + (1 - side if other else side,)

    def copy(self, axis, rank):
        source = self.held[rank].at[self.cut(axis, rank, True)]
        return self.links.send((UNIT, self.name, axis), self.bits[axis], source, self.held[rank + 1])

    def act(self):
        axis = self.order[self.done] if self.done >= 0 else None
        last = self.done == 3
        if axis is None:
            self.first.wait()
            self.held[0][...] += self.kept()
        elif axis == Y:
            self.meeting.wait()
            here, there = self.held[self.rank], self.arrival
        else:
            self.copy(axis, self.rank).wait()
            here, there = self.held[self.rank + 1], self.held[self.rank].at[self.cut(axis, self.rank, False)]
            self.rank += 1
        if axis is not None:
            if last and self.store is not None:
                self.store(here[...].astype(F32) + there[...].astype(F32))
            else:
                here[...] += there[...]
        self.done += 1
        if self.done == 4:
            return
        axis = self.order[self.done]
        if axis != Y:
            self.copy(axis, self.rank).start()
        elif self.arrival is None:
            self.meeting.start()


def pair_up(links, name, keeps, gives):
    rank = keeps.order.index(Y)
    meeting = links.send((UNIT, name, Y), 0, gives.held[rank], keeps.arrival)
    keeps.meeting = gives.meeting = meeting


def arrival_shape(order):
    before = order[: order.index(Y)]
    return [2] * (3 - len(before))


def layer_kernel(
    dp,
    x_hbm, c_hbm, ids_hbm, g1_hbm, b1_hbm, g2_hbm, b2_hbm, qkv_hbm, ow_hbm, up_hbm, dw_hbm,
    out_hbm, ig_hbm, qg_hbm, pgt_hbm, ug_hbm, dgt_hbm, ng_hbm,
    sems, qg_ref, pgt_ref, ug_ref, dgt_ref, wq, wo, wu, wd, g1, b1, g2, b2, ids_ref, xw, cw, na_full, nat, jt, mixt, lses, deltas, lse_full,
    bias, nbt, ct, gmt, mid, acc, gacc, shared_in, shared_out, norms, g_unit, g_out, g_qkv, *landings,
):
    top = dp // 16
    near_bits = NEAR_BITS
    c_bit = top
    axis_bits = {X: 2 * top, Z: 4 * top, ZZ: 8 * top}
    links = Links(sems, [0] + sorted({*near_bits, c_bit, *axis_bits.values()}))
    links.greet()
    me, side = links.me, links.side
    rows_all, width = xw.shape
    heads_width = jt.shape[2]
    tiles = wd.shape[1]
    heads = heads_width // HD
    first = pl.multiple_of(LOW * side, 128)
    window = pl.ds(first, WIN)
    window_there = pl.ds(pl.multiple_of(LOW * (1 - side), 128), WIN)
    at_c = half_index(me, c_bit)

    feed_rows = pl.ds(pl.multiple_of(MID * side, 128), MID)
    feed_in_window = pl.ds(pl.multiple_of(HALF_IMG * side, 128), MID)
    feed_there = pl.ds(pl.multiple_of(MID * (1 - side), 128), MID)

    small = ((ids_hbm, ids_ref), (g1_hbm, g1), (b1_hbm, b1), (g2_hbm, g2), (b2_hbm, b2))
    loads = {"x": links.fetch("x", x_hbm, xw)}
    for n, (source, target) in enumerate(small):
        loads[n] = links.fetch(n, source, target)
    for j in range(3):
        loads["q", j] = links.fetch(("q", j), qkv_hbm.at[j], wq.at[0, j])
    loads["c"] = links.fetch("c", c_hbm.at[feed_rows], cw)
    late = {"o": links.fetch("o", ow_hbm, wo.at[0])}
    for tile in range(tiles):
        cols = pl.ds(tile * TILE, TILE)
        late["u", tile] = links.fetch(("u", tile), up_hbm.at[:, :, :, cols], wu.at[0, :, :, :, cols])
        late["d", tile] = links.fetch(("d", tile), dw_hbm.at[tile], wd.at[0, tile])
    for load in loads.values():
        load.start()

    chunks = {
        OUT: Chunk(links, OUT, near_bits, ow_hbm, wo.at[1], 0),
        QKV: Chunk(links, QKV, near_bits, qkv_hbm, wq.at[1], 1),
    }
    for tile in range(tiles):
        cols = pl.ds(tile * TILE, TILE)
        name = UP + tile
        chunks[name] = Chunk(links, name, near_bits, up_hbm.at[:, :, :, cols], wu.at[1, :, :, :, cols], 0)
        name = DOWN + tile
        chunks[name] = Chunk(links, name, near_bits, dw_hbm.at[tile], wd.at[1, tile], 0)

    blocks = {}
    merges = [None, None]
    norm_count = [0]

    def run(point):
        for action, which in PLAN.get(point, ()):
            if action == UNIT:
                blocks[which].act()
            elif action == MERGE:
                merges[which]()
            elif action == NORM:
                norm_step()
            else:
                chunks[which].act(action)

    links.meet()
    for name in FIRST:
        chunks[name].copy(SIDE).start()

    for n in range(len(small)):
        loads[n].wait()
    ids = ids_ref[...]
    columns = ids.T
    row_ids = jnp.concatenate([ids[i : i + 1] for i in range(rows_all // 128)], axis=1)
    column_ids = jnp.concatenate([columns[:, i : i + 1] for i in range(rows_all // 128)], axis=0)
    low = side == 0
    middle_id = ids[MID // 128 : MID // 128 + 1, 0:1]
    begins = jnp.sum(jnp.where(ids < middle_id, 1.0, 0.0), axis=(0, 1), keepdims=True)
    ends = jnp.sum(jnp.where(ids <= middle_id, 1.0, 0.0), axis=(0, 1), keepdims=True)
    split = jnp.where(MID - begins <= ends - MID, begins, ends)
    sign = jnp.where(low, 1.0, -1.0)
    position = lax.broadcasted_iota(jnp.int32, (1, WIN), 1).astype(F32) + (LOW * side).astype(F32)
    owned_row = jnp.where((position + 0.5 - split) * sign < 0, 1.0, 0.0)

    half_tile = 2 * HALF_IMG
    biases = (
        (acc.at[0:MID, 0:half_tile],),
        (gacc.at[0:MID, 0:half_tile], gacc.at[0:half_tile, half_tile : 2 * half_tile]),
        (mid.at[0:MID, 0:half_tile], mid.at[0:half_tile, half_tile : 2 * half_tile]),
        (acc.at[0:MID, half_tile : 2 * half_tile],),
    )
    for parts, (t0, tn, s0, sn) in zip(biases, BANDS):
        for part in parts:
            s1 = s0 + part.shape[0]
            part[...] = jnp.where(column_ids[s0:s1] == row_ids[:, t0 : t0 + tn], 0.0, MASKED)
            s0 = s1

    def row(ref):
        return ref[...].reshape(1, width)

    def weight(ref):
        value = ref[...]
        return value.reshape(-1, value.shape[-1])

    def in_unit(index):
        return g_unit.at[index // 2, index % 2]

    def head_at(ref, head):
        return ref.at[head // 4, (head // 2) % 2, head % 2]

    pairs = heads // 2

    def mixed_copy(pair):
        here = in_unit(3).at[pair // 2, pair % 2, :, :, feed_there]
        return links.send("m", 0, here, mixt.at[pl.ds(heads + 2 * pair, 2)], number=pair, many=pairs)

    lse_copy = links.send("l", 0, lse_full.at[:, :, window_there], lses.at[pl.ds(heads, heads)])

    def attend(head):
        q = head_at(in_unit(0), head)[...]
        k = head_at(in_unit(1), head)[...].T
        v = jnp.concatenate([head_at(in_unit(2), head)[...], jnp.ones((16, rows_all), BF16)], axis=0)
        for parts, (t0, tn, s0, sn) in zip(biases, BANDS):
            added = jnp.concatenate([part[...] for part in parts], axis=0)
            st = dot(k[s0 : s0 + sn], q[:, t0 : t0 + tn], 1, 0) * SCALE2 + added
            most = jnp.max(st, axis=0, keepdims=True)
            expo = jnp.exp2(st - most)
            res = dot(expo.astype(BF16), v[:, s0 : s0 + sn], 0, 1).T
            total = res[HD : HD + 1]
            head_at(in_unit(3), head)[:, t0 : t0 + tn] = (res[:HD] * (1.0 / total)).astype(BF16)
            lse_full[head, :, t0 : t0 + tn] = most + jnp.log2(total)

    loads["x"].wait()
    xh, unused = standardize(xw[...].astype(F32))
    na_full[...] = (xh * row(g1) + row(b1)).astype(BF16)
    for j in range(3):
        loads["q", j].wait()
    run(LOADED)
    for j in range(3):
        part = dot(weight(wq.at[0, j]), na_full[...], 0, 1).astype(BF16)
        in_unit(j)[...] = part.reshape(2, 2, 2, HD, rows_all)
    for load in late.values():
        load.start()
    run(PROJECTED)
    for head in range(heads // 2):
        attend(head)
    for pair in range(pairs // 2):
        mixed_copy(pair).start()
    run(FORWARD)

    @pl.loop(pairs // 2, pairs)
    def _(pair):
        attend(2 * pair)
        attend(2 * pair + 1)
        mixed_copy(pair).start()
        for number in range(pairs // 2, pairs):

            @pl.when(pair == number)
            def _():
                run(FORWARD + number)

    lse_copy.start()
    for name in SECOND:
        chunks[name].copy(SIDE).start()
    loads["c"].wait()
    ct[...] = cw[...].T
    nat[...] = na_full[window, :].T
    row_ids = jnp.where(low, row_ids[:, :WIN], row_ids[:, LOW:])
    column_ids = jnp.where(low, column_ids[:WIN], column_ids[LOW:])
    bias[...] = jnp.where(column_ids == row_ids, 0.0, MASKED)
    for j in range(3):
        jt[0, j] = in_unit(j)[:, :, :, :, window].reshape(heads_width, WIN)
    mixt[0:heads] = in_unit(3)[:, :, :, :, feed_rows].reshape(heads, HD, MID)
    lses[0:heads] = lse_full[:, :, window]
    run(PREPARED)
    run(NEED + 9)
    late["o"].wait()
    for pair in range(pairs):
        mixed_copy(pair).wait()
    run(MIXED)

    def mixed_rows(half):
        return mixt[half * heads : (half + 1) * heads].reshape(heads_width, MID)

    fed = na_full.at[0:MID]
    middle = mid.at[feed_in_window]
    branch = dot(mixed_rows(0), weight(wo.at[0]), 0, 0) + dot(mixed_rows(1), weight(wo.at[1]), 0, 0)
    acc[...] = xw[feed_rows, :].astype(F32) + branch
    middle[...] = acc[...]
    xh, unused = standardize(acc[...])
    fed[...] = (xh * row(g2) + row(b2)).astype(BF16)
    nbt[...] = fed[...].T
    gacc[...] = jnp.zeros_like(gacc)
    for key, load in late.items():
        if key != "o":
            load.wait()

    unit = g_unit.shape[-1]
    f0, landings = landings[0], list(landings[1:])
    grid = (2, 2, 2, 2, width // 16)

    def block(name, pair, keeps, first_copy, kept, store, held0=None):
        held = [held0] if held0 is not None else [landings.pop(0)]
        held += [landings.pop(0) for _ in range(3)]
        arrival = landings.pop(0) if keeps else None
        blocks[name] = Block(
            links, name, ORDERS[pair], axis_bits, held, arrival, first_copy, kept, store if keeps else None
        )

    def unit_copy(u):
        return links.send("g", c_bit, g_unit.at[u % 2, :, :, :, 1 - at_c], f0.at[u], number=u, many=2 * tiles)

    def unit_results(tile):
        cols = pl.ds(tile * TILE, TILE)
        return [
            links.fetch((tile, "u"), ug_ref.at[:, cols], ug_hbm.at[:, cols]),
            links.fetch((tile, "d"), dgt_ref.at[:, cols], dgt_hbm.at[:, cols]),
        ]

    def unit_store(tile, total):
        cols = slice(tile * TILE, (tile + 1) * TILE)
        ug_ref[:, cols] = total[:, :TILE]
        dgt_ref[:, cols] = total[:, TILE:]
        for copy in unit_results(tile):
            copy.start()

    def out_copy(half):
        return links.send("h", c_bit, g_out.at[half, :, :, :, 1 - at_c], blocks[OUT_BLOCKS + half].held[0], half, 2)

    def out_store(total):
        pgt_ref[...] = total
        links.fetch("p", pgt_ref, pgt_hbm).start()

    columns_back = UNROLL * HD

    def qkv_copy(g):
        return links.send("k", c_bit, g_qkv.at[SEQUENCE.index(g) % 2, :, :, :, 1 - at_c], blocks[QKV_BLOCKS + g].held[0], g, 4)

    def qkv_store(group, total):
        for j in range(3):
            cols = slice(j * columns_back, (j + 1) * columns_back)
            qg_ref[j, :, group * columns_back : (group + 1) * columns_back] = total[:, cols]

    for u in range(2 * tiles):
        kept = functools.partial(lambda u: g_unit[u % 2, :, :, :, at_c], u)
        store = functools.partial(unit_store, u // 2)
        block(u, u // 2, feed_half(u) == 0, unit_copy(u), kept, store, f0.at[u])
    for half in range(2):
        kept = functools.partial(lambda half: g_out[half, :, :, :, at_c], half)
        block(OUT_BLOCKS + half, tiles, half == 0, None, kept, out_store)
        blocks[OUT_BLOCKS + half].first = out_copy(half)
    for g in range(4):
        kept = functools.partial(lambda slot: g_qkv[slot, :, :, :, at_c], SEQUENCE.index(g) % 2)
        block(QKV_BLOCKS + g, tiles + 1 + g % 2, g >= 2, None, kept, functools.partial(qkv_store, g % 2))
        blocks[QKV_BLOCKS + g].first = qkv_copy(g)
    for tile in range(tiles):
        pair = [blocks[2 * tile], blocks[2 * tile + 1]]
        pair_up(links, tile, pair[feed_half(2 * tile)], pair[1 - feed_half(2 * tile)])
    pair_up(links, tiles, blocks[OUT_BLOCKS], blocks[OUT_BLOCKS + 1])
    for g in range(2):
        pair_up(links, tiles + 1 + g, blocks[QKV_BLOCKS + g + 2], blocks[QKV_BLOCKS + g])

    run(READY)

    @pl.loop(0, 2 * tiles)
    def _(u):
        half, tile = feed_half(u), u // 2
        cols = pl.ds(pl.multiple_of(tile * TILE, TILE), TILE)
        for number in [v for v in range(2 * tiles) if feed_half(v)]:

            @pl.when(u == number)
            def _():
                run(NEED + number)

        up = weight(wu.at[half, :, :, :, cols])
        down = weight(wd.at[half, tile])
        hid = dot(fed[...], up, 1, 0)
        phi_sum, phi = normal_parts(hid)
        active = (hid * phi_sum).astype(BF16)
        grad_active = dot(cw[...], down, 1, 1)
        acc[...] += dot(active, down, 1, 0)
        grad_hidden = (grad_active * (phi_sum + hid * phi)).astype(BF16)
        for number in range(2 * tiles):

            @pl.when(u == number)
            def _():
                run(MIDWAY + number)

        slot = u % 2
        g_unit[slot, :, :, :, :, :, TILE:] = dot(ct[...], active, 1, 0).astype(BF16).reshape(*grid, TILE)
        g_unit[slot, :, :, :, :, :, :TILE] = dot(nbt[...], grad_hidden, 1, 0).astype(BF16).reshape(*grid, TILE)
        unit_copy(u).start()
        gacc[...] += dot(grad_hidden, up, 1, 1)
        for number in range(2 * tiles):

            @pl.when(u == number)
            def _():
                run(FEED + number)

    fed[...] = acc[...].astype(BF16)
    xh, inverse = standardize(middle[...])
    grad = gacc[...]
    norms[0, 2:3, :] = jnp.sum(grad * xh, axis=0, keepdims=True)
    norms[0, 3:4, :] = jnp.sum(grad, axis=0, keepdims=True)
    middle[...] = cw[...].astype(F32) + norm_input_grad(xh, inverse, grad, row(g2))
    cw[...] = middle[...].astype(BF16)
    edge_here = pl.ds(pl.multiple_of((MID - HALF_IMG) - 2 * HALF_IMG * side, 128), HALF_IMG)
    edge_there = pl.ds(pl.multiple_of(MID * side, 128), HALF_IMG)
    other_edge = pl.ds(pl.multiple_of(MID * (1 - side), 128), HALF_IMG)
    for half in range(2):
        part = slice(half * heads_width, (half + 1) * heads_width)
        grads = dot(weight(wo.at[half]), cw[...], 1, 1).astype(BF16)
        gmt[part, feed_in_window] = grads
        sums = jnp.sum((grads.astype(F32) * mixed_rows(half).astype(F32)).reshape(heads, HD, MID), axis=1, keepdims=True)
        deltas[half * heads : (half + 1) * heads, :, feed_in_window] = sums
    edge_copies = []
    for half in range(2):
        here, there = (pl.ds(n * heads_width, heads_width) for n in (half, 1 - half))
        edge_copies.append(links.send("e", 0, gmt.at[here, edge_here], gmt.at[there, edge_there], number=half, many=2))
        here, there = (pl.ds(n * heads, heads) for n in (half, 1 - half))
        edge_copies.append(
            links.send("n", 0, deltas.at[here, :, edge_here], deltas.at[there, :, edge_there], number=half, many=2)
        )
    out_copies = [
        links.send("r", 0, fed, out_hbm.at[feed_rows]),
        links.fetch("s", fed, out_hbm.at[feed_rows]),
    ]
    for copy in edge_copies + out_copies:
        copy.start()
    run(SECOND_NORM)
    ct[...] = cw[...].T
    for half in range(2):
        g_out[half] = dot(ct[...], mixed_rows(half), 1, 1).astype(BF16).reshape(*grid, heads_width)
        out_copy(half).start()
    run(SECOND_NORM + 1)
    for copy in edge_copies:
        copy.wait()
    lse_copy.wait()
    deltas[...] = deltas[...] * owned_row
    gmt[...] = (gmt[...].astype(F32) * owned_row).astype(BF16)
    mid[other_edge, :] = jnp.zeros((HALF_IMG, width), F32)
    run(SECOND_NORM + 2)

    def attend_back(half, group):
        for u in range(UNROLL):
            head = group * UNROLL + u
            rows = pl.ds(pl.multiple_of(head * HD, 16), HD)
            out_rows = pl.ds(pl.multiple_of(half * heads_width + head * HD, 16), HD)
            q = jt[half, 0, rows, :]
            k = jt[half, 1, rows, :]
            v = jt[half, 2, rows, :]
            do = gmt[out_rows, :]
            delta = deltas[half * heads + head]
            lse = lses[half * heads + head]
            kt, vt = k.T, v.T
            grads = []
            for s0, sn, t0, tn in BANDS_BACK:
                ss, ts = slice(s0, s0 + sn), slice(t0, t0 + tn)
                st = dot(kt[ss], q[:, ts], 1, 0) * SCALE2 + (bias[ss, ts] - lse[:, ts])
                p = jnp.exp2(st)
                dprobs = dot(vt[ss], do[:, ts], 1, 0)
                ds = (p * (dprobs - delta[:, ts])).astype(BF16)
                grads.append(ds)
                jt[half, 2, rows, ss] = dot(p.astype(BF16), do[:, ts], 1, 1).astype(BF16).T
                jt[half, 1, rows, ss] = (dot(ds, q[:, ts], 1, 1) * SCALE).astype(BF16).T
            for q0, qn, unused, unused in BANDS_BACK:
                total = None
                for ds, (s0, sn, t0, tn) in zip(grads, BANDS_BACK):
                    if t0 <= q0 and q0 + qn <= t0 + tn:
                        part = dot(k[:, s0 : s0 + sn], ds[:, q0 - t0 : q0 - t0 + qn], 1, 0)
                        total = part if total is None else total + part
                jt[half, 0, rows, q0 : q0 + qn] = (total * SCALE).astype(BF16)

    def weight_grad(n):
        half, group = back_step(n)
        rows = pl.ds(pl.multiple_of(group * columns_back, 16), columns_back)
        grads = jnp.concatenate([jt[half, j, rows, :] for j in range(3)], axis=0)
        g_qkv[n % 2] = dot(nat[...], grads, 1, 1).astype(BF16).reshape(*grid, 3 * columns_back)

    first_other = min(SEQUENCE.index(0), SEQUENCE.index(1))

    @pl.loop(0, 4)
    def _(n):
        @pl.when(n == first_other)
        def _():
            run(OTHER)
            for j in range(3):
                jt[1, j] = dot(weight(wq.at[1, j]), nat[...], 0, 0).astype(BF16)

        attend_back(*back_step(n))

        @pl.when(n < 3)
        def _():
            weight_grad(n)

        for number in range(4):

            @pl.when(n == number)
            def _():
                if number < 3:
                    qkv_copy(SEQUENCE[number]).start()
                run(BACK + number)

    for copy in out_copies:
        copy.wait()
    na = na_full.at[0:WIN]
    common_rows = pl.multiple_of(LOW * (1 - side), 128), WIN - LOW
    single_rows = pl.multiple_of((WIN - LOW) * side, 128), LOW
    common, single = pl.ds(*common_rows), pl.ds(*single_rows)
    single_there = pl.ds(pl.multiple_of(WIN * side, 128), LOW)
    ig_common = links.send("i", 0, na.at[common], shared_in)
    ig_copies = [
        links.send("j", 0, na.at[single], ig_hbm.at[single_there]),
        links.fetch("t", na.at[single], ig_hbm.at[single_there]),
        links.fetch("v", shared_out, ig_hbm.at[pl.ds(LOW, WIN - LOW)]),
    ]

    def merge():
        ig_common.wait()
        shared_out[...] = na[common, :] + shared_in[...]
        ig_copies[2].start()

    merges[1] = merge

    def input_grad(start, count):
        rows = pl.ds(start, count)
        grad = None
        for half in range(2):
            for j in range(3):
                part = dot(jt[half, j, :, rows], weight(wq.at[half, j]), 0, 1)
                grad = part if grad is None else grad + part
        xh, inverse = standardize(xw[pl.ds(pl.multiple_of(first + start, 128), count), :].astype(F32))
        na[rows, :] = (mid[rows, :] + norm_input_grad(xh, inverse, grad, row(g1))).astype(BF16)
        return jnp.sum(grad * xh, axis=0, keepdims=True), jnp.sum(grad, axis=0, keepdims=True)

    norm_bits = (c_bit, *axis_bits.values(), 0)

    def norm_copy(n):
        return links.send("w", norm_bits[n], norms.at[2 * n], norms.at[2 * n + 1], number=n, many=5)

    def norm_step():
        n = norm_count[0]
        norm_count[0] += 1
        norm_copy(n).wait()
        norms[2 * n + 2] = norms[2 * n] + norms[2 * n + 1]
        if n < 4:
            norm_copy(n + 1).start()

    weight_grad(3)
    qkv_copy(SEQUENCE[3]).start()
    gain_one, shift_one = input_grad(*common_rows)
    ig_common.start()
    run(TAIL)
    gain_two, shift_two = input_grad(*single_rows)
    for copy in ig_copies[:2]:
        copy.start()
    run(TAIL + 1)
    norms[0, 0:1, :] = gain_one + gain_two
    norms[0, 1:2, :] = shift_one + shift_two
    norms[0, 4:8, :] = jnp.zeros((4, width), F32)
    norm_copy(0).start()
    run(TAIL + 2)
    last_copies = [links.fetch("y", norms.at[10], ng_hbm), links.fetch("z", qg_ref, qg_hbm)]
    for copy in last_copies:
        copy.start()
    for tile in range(tiles):
        for copy in unit_results(tile):
            copy.wait()
    links.fetch("p", pgt_ref, pgt_hbm).wait()
    for copy in last_copies + ig_copies:
        copy.wait()


def collect_kernel(*refs):
    count = (len(refs) - 5) // 3
    sources, norms, targets = refs[:count], refs[count], refs[count + 1 : 2 * count + 1]
    target, held = refs[2 * count + 1], refs[2 * count + 2 : 3 * count + 2]
    norms_held, target_held, sems = refs[3 * count + 2 :]
    loads, stores = [], []
    for source, between, end in zip(sources, held, targets):
        parts = 4 if source.shape[0] % 64 == 0 else 1
        size = source.shape[0] // parts
        for part in range(parts):
            rows, n = pl.ds(part * size, size), len(loads)
            loads.append(pltpu.make_async_copy(source.at[rows], between.at[rows], sems.at[0, n]))
            stores.append(pltpu.make_async_copy(between.at[rows], end.at[rows], sems.at[1, n]))
    load_norms = pltpu.make_async_copy(norms, norms_held, sems.at[0, len(loads)])
    store_norms = pltpu.make_async_copy(target_held, target, sems.at[1, len(loads)])
    load_norms.start()
    for load in loads:
        load.start()
    rows, share = target.shape
    width = norms.shape[1]
    place = lax.broadcasted_iota(jnp.int32, (width, share), 0) - share * lax.axis_index("dp")
    pick = jnp.where(place == lax.broadcasted_iota(jnp.int32, (width, share), 1), 1.0, 0.0)
    load_norms.wait()
    target_held[...] = lax.dot_general(
        norms_held[...], pick, (((1,), (0,)), ((), ())), precision=lax.Precision.HIGHEST, preferred_element_type=F32
    )[:rows]
    store_norms.start()
    for load, store in zip(loads, stores):
        load.wait()
        store.start()
    for store in stores + [store_norms]:
        store.wait()


def local(
    dp,
    block_input,
    segment_ids,
    gain_one,
    shift_one,
    qkv_weight,
    out_weight,
    gain_two,
    shift_two,
    up_weight,
    down_weight,
    out_cotangent,
):
    rows, width = block_input.shape
    heads_width, hidden = out_weight.shape[0], up_weight.shape[1]
    block, unit, group, tiles = width // 16, 2 * TILE, 3 * UNROLL * HD, hidden // TILE
    heads = heads_width // HD
    S, V = jax.ShapeDtypeStruct, pltpu.VMEM
    far = pl.BlockSpec(memory_space=pl.ANY)
    halves = [2, 2, 2, 2]
    landings = [V((2 * tiles, *halves[1:], block, unit), BF16)]
    kinds = [(u // 2, feed_half(u) == 0, unit, False) for u in range(2 * tiles)]
    kinds += [(tiles, half == 0, heads_width, True) for half in range(2)]
    kinds += [(tiles + 1 + g % 2, g >= 2, group, True) for g in range(4)]
    for pair, keeps, wide, whole in kinds:
        landings += [V((*halves[n:], block, wide), BF16) for n in range(1 if whole else 2, 5)]
        if keeps:
            landings.append(V((*arrival_shape(ORDERS[pair]), block, wide), BF16))
    out, ig, qg, pgt, ug, dgt, ng = pl.pallas_call(
        functools.partial(layer_kernel, dp),
        out_shape=(
            S((rows, width), BF16),
            S((rows, width), BF16),
            S((3, block, heads_width), F32),
            S((block, heads_width), F32),
            S((block, hidden), F32),
            S((block, hidden), F32),
            S((8, width), F32),
        ),
        in_specs=[far] * 11,
        out_specs=[far] * 7,
        scratch_shapes=[
            pltpu.SemaphoreType.DMA((SEMAPHORES,)),
            V((3, block, heads_width), F32),
            V((block, heads_width), F32),
            V((block, hidden), F32),
            V((block, hidden), F32),
            V((2, 3, 4, 2, width // 8, heads_width), BF16),
            V((2, 4, 2, heads_width // 8, width), BF16),
            V((2, 4, 2, width // 8, hidden), BF16),
            V((2, tiles, 4, 2, TILE // 8, width), BF16),
            *[V((width,), F32)] * 4,
            V((rows // 128, 128), jnp.int32),
            V((rows, width), BF16),
            V((MID, width), BF16),
            V((rows, width), BF16),
            V((width, WIN), BF16),
            V((2, 3, heads_width, WIN), BF16),
            V((2 * heads, HD, MID), BF16),
            V((2 * heads, 1, WIN), F32),
            V((2 * heads, 1, WIN), F32),
            V((heads, 1, rows), F32),
            V((WIN, WIN), F32),
            V((width, MID), BF16),
            V((width, MID), BF16),
            V((width, WIN), BF16),
            V((WIN, width), F32),
            V((MID, width), F32),
            V((MID, width), F32),
            V((WIN - LOW, width), BF16),
            V((WIN - LOW, width), BF16),
            V((11, 8, width), F32),
            V((2, *halves, block, unit), BF16),
            V((2, *halves, block, heads_width), BF16),
            V((2, *halves, block, group), BF16),
            *landings,
        ],
        compiler_params=pltpu.CompilerParams(
            vmem_limit_bytes=VMEM_LIMIT, collective_id=0, has_side_effects=True
        ),
        name="layer",
    )(
        block_input,
        out_cotangent,
        segment_ids.reshape(rows // 128, 128),
        gain_one,
        shift_one,
        gain_two,
        shift_two,
        qkv_weight.transpose(1, 0, 2).reshape(3, 4, 2, width // 8, heads_width),
        out_weight.reshape(4, 2, heads_width // 8, width),
        up_weight.reshape(4, 2, width // 8, hidden),
        down_weight.reshape(tiles, 4, 2, TILE // 8, width),
    )
    rest = dp // 16
    if rest > 1:
        groups = [list(range(g * rest, (g + 1) * rest)) for g in range(16)]
        scatter = functools.partial(lax.psum_scatter, axis_name="dp", axis_index_groups=groups, tiled=True)
        qg = scatter(qg, scatter_dimension=1)
        pgt, ug, dgt = (scatter(part, scatter_dimension=0) for part in (pgt, ug, dgt))
        ng = lax.psum(ng, "dp", axis_index_groups=groups)
    share = width // dp
    results = (out, ig, qg, pgt, ug, dgt)
    out, ig, qg, pgt, ug, dgt, ng = pl.pallas_call(
        collect_kernel,
        out_shape=tuple(S(a.shape, a.dtype) for a in results) + (S((4, share), F32),),
        in_specs=[far] * 7,
        out_specs=[far] * 7,
        scratch_shapes=[V(a.shape, a.dtype) for a in results]
        + [V(ng.shape, F32), V((4, share), F32), pltpu.SemaphoreType.DMA((2, 24))],
        name="collect",
    )(*results, ng)
    return out, ig, qg.transpose(1, 0, 2), pgt.T, ug, dgt.T, ng


def solution(mesh):
    in_specs = (
        P("dp", None),
        P("dp"),
        P(),
        P(),
        P(None, None, "tp"),
        P("tp", None),
        P(),
        P(),
        P(None, "tp"),
        P("tp", None),
        P("dp", None),
    )
    out_specs = (
        P("dp", None),
        P("dp", None),
        P("dp", None, "tp"),
        P("tp", "dp"),
        P("dp", "tp"),
        P("tp", "dp"),
        P(None, "dp"),
    )
    step = functools.partial(local, mesh.shape["dp"])
    return jax.shard_map(step, mesh=mesh, in_specs=in_specs, out_specs=out_specs, check_vma=False)
```

```python
import functools

import jax
import jax.numpy as jnp
import numpy as np
from jax import lax
from jax.experimental import pallas as pl
from jax.experimental.pallas import tpu as pltpu
from jax.sharding import PartitionSpec as P

HD = 48
SEQ = 1024
IMG = 256
MID = SEQ // 2
HALF_IMG = IMG // 2
WIN = MID + HALF_IMG
LOW = MID - HALF_IMG
EPSILON = 1e-05
MASKED = -1e30
F32 = jnp.float32
BF16 = jnp.bfloat16
SCALE = float(HD ** (-0.5))
SCALE2 = float(HD ** (-0.5) * np.log2(np.e))
HALF_LOG2E = float(0.5 * np.log2(np.e))
INV_SQRT_2PI = 0.3989422804014327
PHI = (
    0.11962326238213554,
    0.12084553903880502,
    0.09934703796123681,
    0.13041684726157698,
    -0.05716832560524514,
    0.21011968093231104,
    -0.1593792042147725,
    0.036195106181360036,
)
TILE = 512
UNROLL = 4
UNROLL_FORWARD = 2
BANDS = ((0, 256, 0, 512), (256, 256, 0, 768), (512, 256, 256, 768), (768, 256, 512, 512))
BANDS_BACK = ((0, 256, 0, 512), (256, 256, 0, 640), (512, 128, 256, 384))
VMEM_LIMIT = 63 << 20
SEMAPHORES = 320
X, Z, ZZ, Y = range(4)
AXES = (ZZ, Z, X)
SIDE, WIDE, DEEP, CROSS, NEAR, UNIT, MERGE, NORM = range(8)
OUT, QKV, UP, DOWN = 0, 1, 2, 5
OUT_BLOCKS, QKV_BLOCKS = 6, 8
FIRST = (OUT, UP, DOWN, UP + 1, DOWN + 1)
SECOND = (UP + 2, DOWN + 2, QKV)
NEAR_BITS = (1, 4, 2)
LOADED, PROJECTED, PREPARED, MIXED, READY, OTHER = range(6)
FORWARD, NEED, MIDWAY, FEED, SECOND_NORM, BACK, TAIL = 10, 20, 30, 40, 50, 60, 70


def dot(a, b, ca, cb):
    return lax.dot_general(a, b, (((ca,), (cb,)), ((), ())), preferred_element_type=F32)


def standardize(values):
    centre = values - jnp.mean(values, axis=-1, keepdims=True)
    inverse = lax.rsqrt(jnp.mean(centre * centre, axis=-1, keepdims=True) + EPSILON)
    return centre * inverse, inverse


def norm_input_grad(xh, inverse, grad, gain):
    dhg = grad * gain
    return inverse * (
        dhg - jnp.mean(dhg, axis=-1, keepdims=True) - xh * jnp.mean(dhg * xh, axis=-1, keepdims=True)
    )


def normal_parts(u):
    t = 1.0 / (1.0 + 0.3 * jnp.abs(u))
    bell = jnp.exp2(u * u * (-HALF_LOG2E))
    poly = PHI[-1]
    for coefficient in PHI[-2::-1]:
        poly = poly * t + coefficient
    tail = poly * t * bell
    return jnp.where(u >= 0, 1.0 - tail, tail), bell * INV_SQRT_2PI
ORDERS = (
    (Y, X, Z, ZZ),
    (X, Z, Y, ZZ),
    (Z, X, Y, ZZ),
    (X, Z, ZZ, Y),
    (X, Y, Z, ZZ),
    (X, Z, ZZ, Y),
)
SEQUENCE = (0, 1, 2, 3)


def back_step(n):
    return 1 - n // 2, n % 2


PLAN = {
    LOADED: ((SIDE, OUT),),
    PROJECTED: ((SIDE, UP), (SIDE, DOWN), (DEEP, OUT)),
    FORWARD: ((SIDE, UP + 1), (DEEP, UP), (SIDE, DOWN + 1)),
    FORWARD + 2: ((DEEP, DOWN), (CROSS, OUT)),
    FORWARD + 3: ((DEEP, UP + 1),),
    PREPARED: ((DEEP, DOWN + 1), (CROSS, UP)),
    NEED + 9: ((NEAR, OUT),),
    READY: ((CROSS, DOWN),),
    MIDWAY + 0: ((SIDE, UP + 2),),
    FEED + 0: ((CROSS, UP + 1), (SIDE, DOWN + 2), (CROSS, DOWN + 1)),
    NEED + 1: ((NEAR, UP), (NEAR, DOWN)),
    MIDWAY + 1: ((DEEP, UP + 2),),
    FEED + 1: ((UNIT, 0), (DEEP, DOWN + 2), (SIDE, QKV)),
    NEED + 2: ((NEAR, UP + 1), (NEAR, DOWN + 1)),
    FEED + 2: ((UNIT, 1), (CROSS, UP + 2)),
    MIDWAY + 3: ((CROSS, DOWN + 2),),
    FEED + 3: ((UNIT, 2), (DEEP, QKV)),
    FEED + 4: ((UNIT, 3),),
    NEED + 5: ((NEAR, UP + 2), (NEAR, DOWN + 2)),
    FEED + 5: ((UNIT, 4), (CROSS, QKV)),
    SECOND_NORM: ((UNIT, 5), (UNIT, 2)),
    SECOND_NORM + 2: ((UNIT, OUT_BLOCKS), (UNIT, OUT_BLOCKS + 1)),
    OTHER: ((NEAR, QKV),),
    BACK + 0: ((UNIT, 4), (UNIT, 3), (UNIT, OUT_BLOCKS), (UNIT, 0), (UNIT, OUT_BLOCKS + 1)),
    BACK + 1: ((UNIT, 5), (UNIT, QKV_BLOCKS), (UNIT, 4), (UNIT, 2)),
    BACK + 2: ((UNIT, QKV_BLOCKS + 1), (UNIT, 3), (UNIT, OUT_BLOCKS), (UNIT, OUT_BLOCKS + 1), (UNIT, 0)),
    BACK + 3: ((UNIT, QKV_BLOCKS + 2), (UNIT, OUT_BLOCKS), (UNIT, 5), (UNIT, OUT_BLOCKS + 1)),
    TAIL: ((UNIT, 3), (UNIT, 0), (UNIT, QKV_BLOCKS), (UNIT, QKV_BLOCKS + 3)),
    TAIL + 1: ((UNIT, 4), (UNIT, OUT_BLOCKS)),
    TAIL + 2: (
        (UNIT, QKV_BLOCKS + 1), (NORM, 0), (UNIT, 3), (UNIT, QKV_BLOCKS + 2), (UNIT, 0), (MERGE, 1),
        (UNIT, QKV_BLOCKS + 3), (UNIT, 4), (NORM, 0), (UNIT, QKV_BLOCKS + 2), (UNIT, QKV_BLOCKS + 1),
        (UNIT, QKV_BLOCKS + 3), (NORM, 0), (UNIT, QKV_BLOCKS + 2), (UNIT, QKV_BLOCKS + 1), (UNIT, QKV_BLOCKS + 3),
        (NORM, 0), (UNIT, QKV_BLOCKS + 2), (UNIT, QKV_BLOCKS + 3), (NORM, 0),
    ),
}


def feed_half(u):
    return (u + 1) // 2 % 2


def half_index(index, bit):
    return (index // bit) % 2


class Links:
    def __init__(self, sems, bits):
        self.sems, self.count, self.known = sems, 0, {}
        self.me, self.side = lax.axis_index("dp"), lax.axis_index("tp")
        self.bits = bits

    def semaphore(self, name, number=0, many=1):
        if name not in self.known:
            self.known[name] = self.count
            self.count += many
        return self.sems.at[self.known[name] + number]

    def partner(self, bit):
        if bit == 0:
            return {"tp": 1 - self.side}
        return {"dp": self.me + bit * (1 - 2 * half_index(self.me, bit))}

    def greet(self):
        barrier = pltpu.get_barrier_semaphore()
        for bit in self.bits:
            pl.semaphore_signal(barrier, inc=1, device_id=self.partner(bit), device_id_type=pl.DeviceIdType.MESH)

    def meet(self):
        pl.semaphore_wait(pltpu.get_barrier_semaphore(), len(self.bits))

    def send(self, name, bit, src, dst, number=0, many=1):
        return pltpu.make_async_remote_copy(
            src_ref=src,
            dst_ref=dst,
            send_sem=self.semaphore((name, 0), number, many),
            recv_sem=self.semaphore((name, 1), number, many),
            device_id=self.partner(bit),
            device_id_type=pl.DeviceIdType.MESH,
        )

    def fetch(self, name, src, dst):
        return pltpu.make_async_copy(src, dst, self.semaphore(name))


class Chunk:
    def __init__(self, links, name, bits, source, target, lead):
        self.links, self.name, self.source, self.target, self.lead = links, name, source, target, lead
        self.core_bit, self.wide_bit, self.deep_bit = bits

    def copy(self, step):
        near, wide, deep = (half_index(self.links.me, b) for b in (self.core_bit, self.wide_bit, self.deep_bit))
        ahead = (slice(None),) * self.lead
        mine = (*ahead, 2 * deep + wide, near)
        bit, where = {
            SIDE: (0, mine),
            WIDE: (self.wide_bit, mine),
            DEEP: (self.deep_bit, mine),
            CROSS: (self.wide_bit, (*ahead, 2 * (1 - deep) + wide, near)),
            NEAR: (self.core_bit, (*ahead, slice(None), near)),
        }[step]
        source = self.source if step == SIDE else self.target
        return self.links.send((step, self.name), bit, source.at[where], self.target.at[where])

    def act(self, step):
        if step == SIDE:
            self.copy(SIDE).wait()
            self.copy(WIDE).start()
            self.copy(DEEP).start()
        elif step == DEEP:
            self.copy(DEEP).wait()
            self.copy(CROSS).start()
        elif step == CROSS:
            self.copy(WIDE).wait()
            self.copy(CROSS).wait()
            self.copy(NEAR).start()
        else:
            self.copy(NEAR).wait()


class Block:
    def __init__(self, links, name, order, bits, held, arrival, first, kept, store):
        self.links, self.name, self.order, self.bits, self.held, self.arrival = links, name, order, bits, held, arrival
        self.first, self.kept, self.store = first, kept, store
        self.done, self.rank, self.meeting = -1, 0, None

    def axes(self, rank):
        return [axis for axis in self.order if axis != Y][:rank]

    def cut(self, axis, rank, other):
        left = [a for a in AXES if a not in self.axes(rank)]
        side = half_index(self.links.me, self.bits[axis])
        return (slice(None),) * left.index(axis) + (1 - side if other else side,)

    def copy(self, axis, rank):
        source = self.held[rank].at[self.cut(axis, rank, True)]
        return self.links.send((UNIT, self.name, axis), self.bits[axis], source, self.held[rank + 1])

    def act(self):
        axis = self.order[self.done] if self.done >= 0 else None
        last = self.done == 3
        if axis is None:
            self.first.wait()
            self.held[0][...] += self.kept()
        elif axis == Y:
            for copy in self.meeting:
                copy.wait()
            here, there = self.held[self.rank], self.arrival
        else:
            self.copy(axis, self.rank).wait()
            here, there = self.held[self.rank + 1], self.held[self.rank].at[self.cut(axis, self.rank, False)]
            self.rank += 1
        if axis is not None:
            if last and self.store is not None:
                self.store(here[...].astype(F32) + there[...].astype(F32))
            else:
                here[...] += there[...]
        self.done += 1
        if self.done == 4:
            return
        axis = self.order[self.done]
        if axis != Y:
            self.copy(axis, self.rank).start()
        elif self.arrival is None:
            self.meeting[0].start()


def pair_up(links, name, keeps, gives):
    rank = keeps.order.index(Y)
    source, target = gives.held[rank], keeps.arrival
    if rank == 0 and name == 0:
        parts = [(source.at[n], target.at[n]) for n in range(2)]
    else:
        parts = [(source, target)]
    meeting = [links.send((UNIT, name, Y), 0, *part, number=n, many=2) for n, part in enumerate(parts)]
    keeps.meeting = gives.meeting = meeting


def arrival_shape(order):
    before = order[: order.index(Y)]
    return [2] * (3 - len(before))


def layer_kernel(
    dp,
    x_hbm, c_hbm, ids_hbm, g1_hbm, b1_hbm, g2_hbm, b2_hbm, qkv_hbm, ow_hbm, up_hbm, dw_hbm,
    out_hbm, ig_hbm, qg_hbm, pgt_hbm, ug_hbm, dgt_hbm, ng_hbm,
    sems, qg_ref, pgt_ref, ug_ref, dgt_ref, wq, wo, wu, wd, g1, b1, g2, b2, ids_ref, xw, cw, na_full, nat, jt, mixt, lses, deltas, lse_full,
    bias, nbt, ct, gmt, mid, acc, gacc, shared_in, shared_out, norms, g_unit, g_out, g_qkv, *landings,
):
    top = dp // 16
    near_bits = NEAR_BITS
    c_bit = top
    axis_bits = {X: 2 * top, Z: 4 * top, ZZ: 8 * top}
    links = Links(sems, [0] + sorted({*near_bits, c_bit, *axis_bits.values()}))
    links.greet()
    me, side = links.me, links.side
    rows_all, width = xw.shape
    heads_width = jt.shape[2]
    tiles = wd.shape[1]
    heads = heads_width // HD
    first = pl.multiple_of(LOW * side, 128)
    window = pl.ds(first, WIN)
    window_there = pl.ds(pl.multiple_of(LOW * (1 - side), 128), WIN)
    at_c = half_index(me, c_bit)

    feed_rows = pl.ds(pl.multiple_of(MID * side, 128), MID)
    feed_in_window = pl.ds(pl.multiple_of(HALF_IMG * side, 128), MID)
    feed_there = pl.ds(pl.multiple_of(MID * (1 - side), 128), MID)

    small = ((ids_hbm, ids_ref), (g1_hbm, g1), (b1_hbm, b1), (g2_hbm, g2), (b2_hbm, b2))
    loads = {"x": links.fetch("x", x_hbm, xw)}
    for n, (source, target) in enumerate(small):
        loads[n] = links.fetch(n, source, target)
    for j in range(3):
        loads["q", j] = links.fetch(("q", j), qkv_hbm.at[j], wq.at[0, j])
    loads["c"] = links.fetch("c", c_hbm.at[feed_rows], cw)
    late = {"o": links.fetch("o", ow_hbm, wo.at[0])}
    for tile in range(tiles):
        cols = pl.ds(tile * TILE, TILE)
        late["u", tile] = links.fetch(("u", tile), up_hbm.at[:, :, :, cols], wu.at[0, :, :, :, cols])
        late["d", tile] = links.fetch(("d", tile), dw_hbm.at[tile], wd.at[0, tile])
    for load in loads.values():
        load.start()

    chunks = {
        OUT: Chunk(links, OUT, near_bits, ow_hbm, wo.at[1], 0),
        QKV: Chunk(links, QKV, near_bits, qkv_hbm, wq.at[1], 1),
    }
    for tile in range(tiles):
        cols = pl.ds(tile * TILE, TILE)
        name = UP + tile
        chunks[name] = Chunk(links, name, near_bits, up_hbm.at[:, :, :, cols], wu.at[1, :, :, :, cols], 0)
        name = DOWN + tile
        chunks[name] = Chunk(links, name, near_bits, dw_hbm.at[tile], wd.at[1, tile], 0)

    blocks = {}
    merges = [None, None]
    norm_count = [0]

    def run(point):
        for action, which in PLAN.get(point, ()):
            if action == UNIT:
                blocks[which].act()
            elif action == MERGE:
                merges[which]()
            elif action == NORM:
                norm_step()
            else:
                chunks[which].act(action)

    links.meet()
    for name in FIRST:
        chunks[name].copy(SIDE).start()

    for n in range(len(small)):
        loads[n].wait()
    ids = ids_ref[...]
    columns = ids.T
    row_ids = jnp.concatenate([ids[i : i + 1] for i in range(rows_all // 128)], axis=1)
    column_ids = jnp.concatenate([columns[:, i : i + 1] for i in range(rows_all // 128)], axis=0)
    low = side == 0
    middle_id = ids[MID // 128 : MID // 128 + 1, 0:1]
    begins = jnp.sum(jnp.where(ids < middle_id, 1.0, 0.0), axis=(0, 1), keepdims=True)
    ends = jnp.sum(jnp.where(ids <= middle_id, 1.0, 0.0), axis=(0, 1), keepdims=True)
    split = jnp.where(MID - begins <= ends - MID, begins, ends)
    sign = jnp.where(low, 1.0, -1.0)
    position = lax.broadcasted_iota(jnp.int32, (1, WIN), 1).astype(F32) + (LOW * side).astype(F32)
    owned_row = jnp.where((position + 0.5 - split) * sign < 0, 1.0, 0.0)

    half_tile = 2 * HALF_IMG
    biases = (
        (acc.at[0:MID, 0:half_tile],),
        (gacc.at[0:MID, 0:half_tile], gacc.at[0:half_tile, half_tile : 2 * half_tile]),
        (mid.at[0:MID, 0:half_tile], mid.at[0:half_tile, half_tile : 2 * half_tile]),
        (acc.at[0:MID, half_tile : 2 * half_tile],),
    )
    for parts, (t0, tn, s0, sn) in zip(biases, BANDS):
        for part in parts:
            s1 = s0 + part.shape[0]
            part[...] = jnp.where(column_ids[s0:s1] == row_ids[:, t0 : t0 + tn], 0.0, MASKED)
            s0 = s1

    def row(ref):
        return ref[...].reshape(1, width)

    def weight(ref):
        value = ref[...]
        return value.reshape(-1, value.shape[-1])

    def in_unit(index):
        return g_unit.at[index // 2, index % 2]

    def head_at(ref, head):
        return ref.at[head // 4, (head // 2) % 2, head % 2]

    pairs = heads // 2

    def mixed_copy(pair):
        here = in_unit(3).at[pair // 2, pair % 2, :, :, feed_there]
        return links.send("m", 0, here, mixt.at[pl.ds(heads + 2 * pair, 2)], number=pair, many=pairs)

    lse_copy = links.send("l", 0, lse_full.at[:, :, window_there], lses.at[pl.ds(heads, heads)])

    def attend(head):
        q = head_at(in_unit(0), head)[...]
        k = head_at(in_unit(1), head)[...].T
        v = jnp.concatenate([head_at(in_unit(2), head)[...], jnp.ones((16, rows_all), BF16)], axis=0)
        for parts, (t0, tn, s0, sn) in zip(biases, BANDS):
            added = jnp.concatenate([part[...] for part in parts], axis=0)
            st = dot(k[s0 : s0 + sn], q[:, t0 : t0 + tn], 1, 0) * SCALE2 + added
            most = jnp.max(st, axis=0, keepdims=True)
            expo = jnp.exp2(st - most)
            res = dot(expo.astype(BF16), v[:, s0 : s0 + sn], 0, 1).T
            total = res[HD : HD + 1]
            head_at(in_unit(3), head)[:, t0 : t0 + tn] = (res[:HD] * (1.0 / total)).astype(BF16)
            lse_full[head, :, t0 : t0 + tn] = most + jnp.log2(total)

    loads["x"].wait()
    xh, unused = standardize(xw[...].astype(F32))
    na_full[...] = (xh * row(g1) + row(b1)).astype(BF16)
    for j in range(3):
        loads["q", j].wait()
    run(LOADED)
    for j in range(3):
        part = dot(weight(wq.at[0, j]), na_full[...], 0, 1).astype(BF16)
        in_unit(j)[...] = part.reshape(2, 2, 2, HD, rows_all)
    for load in late.values():
        load.start()
    run(PROJECTED)
    for head in range(heads // 2):
        attend(head)
    for pair in range(pairs // 2):
        mixed_copy(pair).start()
    run(FORWARD)

    @pl.loop(pairs // 2, pairs)
    def _(pair):
        attend(2 * pair)
        attend(2 * pair + 1)
        mixed_copy(pair).start()
        for number in range(pairs // 2, pairs):

            @pl.when(pair == number)
            def _():
                run(FORWARD + number)

    lse_copy.start()
    for name in SECOND:
        chunks[name].copy(SIDE).start()
    loads["c"].wait()
    ct[...] = cw[...].T
    nat[...] = na_full[window, :].T
    row_ids = jnp.where(low, row_ids[:, :WIN], row_ids[:, LOW:])
    column_ids = jnp.where(low, column_ids[:WIN], column_ids[LOW:])
    bias[...] = jnp.where(column_ids == row_ids, 0.0, MASKED)
    for j in range(3):
        jt[0, j] = in_unit(j)[:, :, :, :, window].reshape(heads_width, WIN)
    mixt[0:heads] = in_unit(3)[:, :, :, :, feed_rows].reshape(heads, HD, MID)
    lses[0:heads] = lse_full[:, :, window]
    run(PREPARED)
    run(NEED + 9)
    late["o"].wait()
    for pair in range(pairs):
        mixed_copy(pair).wait()
    run(MIXED)

    def mixed_rows(half):
        return mixt[half * heads : (half + 1) * heads].reshape(heads_width, MID)

    fed = na_full.at[0:MID]
    middle = mid.at[feed_in_window]
    branch = dot(mixed_rows(0), weight(wo.at[0]), 0, 0) + dot(mixed_rows(1), weight(wo.at[1]), 0, 0)
    acc[...] = xw[feed_rows, :].astype(F32) + branch
    middle[...] = acc[...]
    xh, unused = standardize(acc[...])
    fed[...] = (xh * row(g2) + row(b2)).astype(BF16)
    nbt[...] = fed[...].T
    gacc[...] = jnp.zeros_like(gacc)
    for key, load in late.items():
        if key != "o":
            load.wait()

    unit = g_unit.shape[-1]
    f0, landings = landings[0], list(landings[1:])
    grid = (2, 2, 2, 2, width // 16)

    def block(name, pair, keeps, first_copy, kept, store, held0=None):
        held = [held0] if held0 is not None else [landings.pop(0)]
        held += [landings.pop(0) for _ in range(3)]
        arrival = landings.pop(0) if keeps else None
        blocks[name] = Block(
            links, name, ORDERS[pair], axis_bits, held, arrival, first_copy, kept, store if keeps else None
        )

    def unit_copy(u):
        return links.send("g", c_bit, g_unit.at[u % 2, :, :, :, 1 - at_c], f0.at[u], number=u, many=2 * tiles)

    def unit_results(tile):
        cols = pl.ds(tile * TILE, TILE)
        return [
            links.fetch((tile, "u"), ug_ref.at[:, cols], ug_hbm.at[:, cols]),
            links.fetch((tile, "d"), dgt_ref.at[:, cols], dgt_hbm.at[:, cols]),
        ]

    def unit_store(tile, total):
        cols = slice(tile * TILE, (tile + 1) * TILE)
        ug_ref[:, cols] = total[:, :TILE]
        dgt_ref[:, cols] = total[:, TILE:]
        for copy in unit_results(tile):
            copy.start()

    def out_copy(half):
        return links.send("h", c_bit, g_out.at[half, :, :, :, 1 - at_c], blocks[OUT_BLOCKS + half].held[0], half, 2)

    def out_store(total):
        pgt_ref[...] = total
        links.fetch("p", pgt_ref, pgt_hbm).start()

    columns_back = UNROLL * HD

    def qkv_copy(g):
        return links.send("k", c_bit, g_qkv.at[SEQUENCE.index(g) % 2, :, :, :, 1 - at_c], blocks[QKV_BLOCKS + g].held[0], g, 4)

    def qkv_store(group, total):
        for j in range(3):
            cols = slice(j * columns_back, (j + 1) * columns_back)
            qg_ref[j, :, group * columns_back : (group + 1) * columns_back] = total[:, cols]

    for u in range(2 * tiles):
        kept = functools.partial(lambda u: g_unit[u % 2, :, :, :, at_c], u)
        store = functools.partial(unit_store, u // 2)
        block(u, u // 2, feed_half(u) == 0, unit_copy(u), kept, store, f0.at[u])
    for half in range(2):
        kept = functools.partial(lambda half: g_out[half, :, :, :, at_c], half)
        block(OUT_BLOCKS + half, tiles, half == 0, None, kept, out_store)
        blocks[OUT_BLOCKS + half].first = out_copy(half)
    for g in range(4):
        kept = functools.partial(lambda slot: g_qkv[slot, :, :, :, at_c], SEQUENCE.index(g) % 2)
        block(QKV_BLOCKS + g, tiles + 1 + g % 2, g >= 2, None, kept, functools.partial(qkv_store, g % 2))
        blocks[QKV_BLOCKS + g].first = qkv_copy(g)
    for tile in range(tiles):
        pair = [blocks[2 * tile], blocks[2 * tile + 1]]
        pair_up(links, tile, pair[feed_half(2 * tile)], pair[1 - feed_half(2 * tile)])
    pair_up(links, tiles, blocks[OUT_BLOCKS], blocks[OUT_BLOCKS + 1])
    for g in range(2):
        pair_up(links, tiles + 1 + g, blocks[QKV_BLOCKS + g + 2], blocks[QKV_BLOCKS + g])

    run(READY)

    @pl.loop(0, 2 * tiles)
    def _(u):
        half, tile = feed_half(u), u // 2
        cols = pl.ds(pl.multiple_of(tile * TILE, TILE), TILE)
        for number in [v for v in range(2 * tiles) if feed_half(v)]:

            @pl.when(u == number)
            def _():
                run(NEED + number)

        up = weight(wu.at[half, :, :, :, cols])
        down = weight(wd.at[half, tile])
        hid = dot(fed[...], up, 1, 0)
        phi_sum, phi = normal_parts(hid)
        active = (hid * phi_sum).astype(BF16)
        grad_active = dot(cw[...], down, 1, 1)
        acc[...] += dot(active, down, 1, 0)
        grad_hidden = (grad_active * (phi_sum + hid * phi)).astype(BF16)
        for number in range(2 * tiles):

            @pl.when(u == number)
            def _():
                run(MIDWAY + number)

        slot = u % 2
        g_unit[slot, :, :, :, :, :, TILE:] = dot(ct[...], active, 1, 0).astype(BF16).reshape(*grid, TILE)
        g_unit[slot, :, :, :, :, :, :TILE] = dot(nbt[...], grad_hidden, 1, 0).astype(BF16).reshape(*grid, TILE)
        unit_copy(u).start()
        gacc[...] += dot(grad_hidden, up, 1, 1)
        for number in range(2 * tiles):

            @pl.when(u == number)
            def _():
                run(FEED + number)

    fed[...] = acc[...].astype(BF16)
    xh, inverse = standardize(middle[...])
    grad = gacc[...]
    norms[0, 2:3, :] = jnp.sum(grad * xh, axis=0, keepdims=True)
    norms[0, 3:4, :] = jnp.sum(grad, axis=0, keepdims=True)
    middle[...] = cw[...].astype(F32) + norm_input_grad(xh, inverse, grad, row(g2))
    cw[...] = middle[...].astype(BF16)
    edge_here = pl.ds(pl.multiple_of((MID - HALF_IMG) - 2 * HALF_IMG * side, 128), HALF_IMG)
    edge_there = pl.ds(pl.multiple_of(MID * side, 128), HALF_IMG)
    other_edge = pl.ds(pl.multiple_of(MID * (1 - side), 128), HALF_IMG)
    for half in range(2):
        part = slice(half * heads_width, (half + 1) * heads_width)
        grads = dot(weight(wo.at[half]), cw[...], 1, 1).astype(BF16)
        gmt[part, feed_in_window] = grads
        sums = jnp.sum((grads.astype(F32) * mixed_rows(half).astype(F32)).reshape(heads, HD, MID), axis=1, keepdims=True)
        deltas[half * heads : (half + 1) * heads, :, feed_in_window] = sums
    edge_copies = []
    for half in range(2):
        here, there = (pl.ds(n * heads_width, heads_width) for n in (half, 1 - half))
        edge_copies.append(links.send("e", 0, gmt.at[here, edge_here], gmt.at[there, edge_there], number=half, many=2))
        here, there = (pl.ds(n * heads, heads) for n in (half, 1 - half))
        edge_copies.append(
            links.send("n", 0, deltas.at[here, :, edge_here], deltas.at[there, :, edge_there], number=half, many=2)
        )
    out_copies = [
        links.send("r", 0, fed, out_hbm.at[feed_rows]),
        links.fetch("s", fed, out_hbm.at[feed_rows]),
    ]
    for copy in edge_copies + blocks[0].meeting[1:] + out_copies:
        copy.start()
    run(SECOND_NORM)
    ct[...] = cw[...].T
    for half in range(2):
        g_out[half] = dot(ct[...], mixed_rows(half), 1, 1).astype(BF16).reshape(*grid, heads_width)
        out_copy(half).start()
    run(SECOND_NORM + 1)
    for copy in edge_copies:
        copy.wait()
    lse_copy.wait()
    deltas[...] = deltas[...] * owned_row
    gmt[...] = (gmt[...].astype(F32) * owned_row).astype(BF16)
    mid[other_edge, :] = jnp.zeros((HALF_IMG, width), F32)
    run(SECOND_NORM + 2)

    def attend_back(half, group):
        for u in range(UNROLL):
            head = group * UNROLL + u
            rows = pl.ds(pl.multiple_of(head * HD, 16), HD)
            out_rows = pl.ds(pl.multiple_of(half * heads_width + head * HD, 16), HD)
            q = jt[half, 0, rows, :]
            k = jt[half, 1, rows, :]
            v = jt[half, 2, rows, :]
            do = gmt[out_rows, :]
            delta = deltas[half * heads + head]
            lse = lses[half * heads + head]
            kt, vt = k.T, v.T
            grads = []
            for s0, sn, t0, tn in BANDS_BACK:
                ss, ts = slice(s0, s0 + sn), slice(t0, t0 + tn)
                st = dot(kt[ss], q[:, ts], 1, 0) * SCALE2 + (bias[ss, ts] - lse[:, ts])
                p = jnp.exp2(st)
                dprobs = dot(vt[ss], do[:, ts], 1, 0)
                ds = (p * (dprobs - delta[:, ts])).astype(BF16)
                grads.append(ds)
                jt[half, 2, rows, ss] = dot(p.astype(BF16), do[:, ts], 1, 1).astype(BF16).T
                jt[half, 1, rows, ss] = (dot(ds, q[:, ts], 1, 1) * SCALE).astype(BF16).T
            for q0, qn, unused, unused in BANDS_BACK:
                total = None
                for ds, (s0, sn, t0, tn) in zip(grads, BANDS_BACK):
                    if t0 <= q0 and q0 + qn <= t0 + tn:
                        part = dot(k[:, s0 : s0 + sn], ds[:, q0 - t0 : q0 - t0 + qn], 1, 0)
                        total = part if total is None else total + part
                jt[half, 0, rows, q0 : q0 + qn] = (total * SCALE).astype(BF16)

    def weight_grad(n):
        half, group = back_step(n)
        rows = pl.ds(pl.multiple_of(group * columns_back, 16), columns_back)
        grads = jnp.concatenate([jt[half, j, rows, :] for j in range(3)], axis=0)
        g_qkv[n % 2] = dot(nat[...], grads, 1, 1).astype(BF16).reshape(*grid, 3 * columns_back)

    first_other = min(SEQUENCE.index(0), SEQUENCE.index(1))

    @pl.loop(0, 4)
    def _(n):
        @pl.when(n == first_other)
        def _():
            run(OTHER)
            for j in range(3):
                jt[1, j] = dot(weight(wq.at[1, j]), nat[...], 0, 0).astype(BF16)

        attend_back(*back_step(n))

        @pl.when(n < 3)
        def _():
            weight_grad(n)

        for number in range(4):

            @pl.when(n == number)
            def _():
                if number < 3:
                    qkv_copy(SEQUENCE[number]).start()
                run(BACK + number)

    for copy in out_copies:
        copy.wait()
    na = na_full.at[0:WIN]
    common_rows = pl.multiple_of(LOW * (1 - side), 128), WIN - LOW
    single_rows = pl.multiple_of((WIN - LOW) * side, 128), LOW
    common, single = pl.ds(*common_rows), pl.ds(*single_rows)
    single_there = pl.ds(pl.multiple_of(WIN * side, 128), LOW)
    ig_common = links.send("i", 0, na.at[common], shared_in)
    ig_copies = [
        links.send("j", 0, na.at[single], ig_hbm.at[single_there]),
        links.fetch("t", na.at[single], ig_hbm.at[single_there]),
        links.fetch("v", shared_out, ig_hbm.at[pl.ds(LOW, WIN - LOW)]),
    ]

    def merge():
        ig_common.wait()
        shared_out[...] = na[common, :] + shared_in[...]
        ig_copies[2].start()

    merges[1] = merge

    def input_grad(start, count):
        rows = pl.ds(start, count)
        grad = None
        for half in range(2):
            for j in range(3):
                part = dot(jt[half, j, :, rows], weight(wq.at[half, j]), 0, 1)
                grad = part if grad is None else grad + part
        xh, inverse = standardize(xw[pl.ds(pl.multiple_of(first + start, 128), count), :].astype(F32))
        na[rows, :] = (mid[rows, :] + norm_input_grad(xh, inverse, grad, row(g1))).astype(BF16)
        return jnp.sum(grad * xh, axis=0, keepdims=True), jnp.sum(grad, axis=0, keepdims=True)

    norm_bits = (c_bit, *axis_bits.values(), 0)

    def norm_copy(n):
        return links.send("w", norm_bits[n], norms.at[2 * n], norms.at[2 * n + 1], number=n, many=5)

    def norm_step():
        n = norm_count[0]
        norm_count[0] += 1
        norm_copy(n).wait()
        norms[2 * n + 2] = norms[2 * n] + norms[2 * n + 1]
        if n < 4:
            norm_copy(n + 1).start()

    weight_grad(3)
    qkv_copy(SEQUENCE[3]).start()
    gain_one, shift_one = input_grad(*common_rows)
    ig_common.start()
    run(TAIL)
    gain_two, shift_two = input_grad(*single_rows)
    for copy in ig_copies[:2]:
        copy.start()
    run(TAIL + 1)
    norms[0, 0:1, :] = gain_one + gain_two
    norms[0, 1:2, :] = shift_one + shift_two
    norms[0, 4:8, :] = jnp.zeros((4, width), F32)
    norm_copy(0).start()
    run(TAIL + 2)
    last_copies = [links.fetch("y", norms.at[10], ng_hbm), links.fetch("z", qg_ref, qg_hbm)]
    for copy in last_copies:
        copy.start()
    for tile in range(tiles):
        for copy in unit_results(tile):
            copy.wait()
    links.fetch("p", pgt_ref, pgt_hbm).wait()
    for copy in last_copies + ig_copies:
        copy.wait()


def collect_kernel(*refs):
    count = (len(refs) - 5) // 3
    sources, norms, targets = refs[:count], refs[count], refs[count + 1 : 2 * count + 1]
    target, held = refs[2 * count + 1], refs[2 * count + 2 : 3 * count + 2]
    norms_held, target_held, sems = refs[3 * count + 2 :]
    loads, stores = [], []
    for source, between, end in zip(sources, held, targets):
        parts = 4 if source.shape[0] % 64 == 0 else 1
        size = source.shape[0] // parts
        for part in range(parts):
            rows, n = pl.ds(part * size, size), len(loads)
            loads.append(pltpu.make_async_copy(source.at[rows], between.at[rows], sems.at[0, n]))
            stores.append(pltpu.make_async_copy(between.at[rows], end.at[rows], sems.at[1, n]))
    load_norms = pltpu.make_async_copy(norms, norms_held, sems.at[0, len(loads)])
    store_norms = pltpu.make_async_copy(target_held, target, sems.at[1, len(loads)])
    load_norms.start()
    for load in loads:
        load.start()
    rows, share = target.shape
    width = norms.shape[1]
    place = lax.broadcasted_iota(jnp.int32, (width, share), 0) - share * lax.axis_index("dp")
    pick = jnp.where(place == lax.broadcasted_iota(jnp.int32, (width, share), 1), 1.0, 0.0)
    load_norms.wait()
    target_held[...] = lax.dot_general(
        norms_held[...], pick, (((1,), (0,)), ((), ())), precision=lax.Precision.HIGHEST, preferred_element_type=F32
    )[:rows]
    store_norms.start()
    for load, store in zip(loads, stores):
        load.wait()
        store.start()
    for store in stores + [store_norms]:
        store.wait()


def local(
    dp,
    block_input,
    segment_ids,
    gain_one,
    shift_one,
    qkv_weight,
    out_weight,
    gain_two,
    shift_two,
    up_weight,
    down_weight,
    out_cotangent,
):
    rows, width = block_input.shape
    heads_width, hidden = out_weight.shape[0], up_weight.shape[1]
    block, unit, group, tiles = width // 16, 2 * TILE, 3 * UNROLL * HD, hidden // TILE
    heads = heads_width // HD
    S, V = jax.ShapeDtypeStruct, pltpu.VMEM
    far = pl.BlockSpec(memory_space=pl.ANY)
    halves = [2, 2, 2, 2]
    landings = [V((2 * tiles, *halves[1:], block, unit), BF16)]
    kinds = [(u // 2, feed_half(u) == 0, unit, False) for u in range(2 * tiles)]
    kinds += [(tiles, half == 0, heads_width, True) for half in range(2)]
    kinds += [(tiles + 1 + g % 2, g >= 2, group, True) for g in range(4)]
    for pair, keeps, wide, whole in kinds:
        landings += [V((*halves[n:], block, wide), BF16) for n in range(1 if whole else 2, 5)]
        if keeps:
            landings.append(V((*arrival_shape(ORDERS[pair]), block, wide), BF16))
    out, ig, qg, pgt, ug, dgt, ng = pl.pallas_call(
        functools.partial(layer_kernel, dp),
        out_shape=(
            S((rows, width), BF16),
            S((rows, width), BF16),
            S((3, block, heads_width), F32),
            S((block, heads_width), F32),
            S((block, hidden), F32),
            S((block, hidden), F32),
            S((8, width), F32),
        ),
        in_specs=[far] * 11,
        out_specs=[far] * 7,
        scratch_shapes=[
            pltpu.SemaphoreType.DMA((SEMAPHORES,)),
            V((3, block, heads_width), F32),
            V((block, heads_width), F32),
            V((block, hidden), F32),
            V((block, hidden), F32),
            V((2, 3, 4, 2, width // 8, heads_width), BF16),
            V((2, 4, 2, heads_width // 8, width), BF16),
            V((2, 4, 2, width // 8, hidden), BF16),
            V((2, tiles, 4, 2, TILE // 8, width), BF16),
            *[V((width,), F32)] * 4,
            V((rows // 128, 128), jnp.int32),
            V((rows, width), BF16),
            V((MID, width), BF16),
            V((rows, width), BF16),
            V((width, WIN), BF16),
            V((2, 3, heads_width, WIN), BF16),
            V((2 * heads, HD, MID), BF16),
            V((2 * heads, 1, WIN), F32),
            V((2 * heads, 1, WIN), F32),
            V((heads, 1, rows), F32),
            V((WIN, WIN), F32),
            V((width, MID), BF16),
            V((width, MID), BF16),
            V((width, WIN), BF16),
            V((WIN, width), F32),
            V((MID, width), F32),
            V((MID, width), F32),
            V((WIN - LOW, width), BF16),
            V((WIN - LOW, width), BF16),
            V((11, 8, width), F32),
            V((2, *halves, block, unit), BF16),
            V((2, *halves, block, heads_width), BF16),
            V((2, *halves, block, group), BF16),
            *landings,
        ],
        compiler_params=pltpu.CompilerParams(
            vmem_limit_bytes=VMEM_LIMIT, collective_id=0, has_side_effects=True
        ),
        name="layer",
    )(
        block_input,
        out_cotangent,
        segment_ids.reshape(rows // 128, 128),
        gain_one,
        shift_one,
        gain_two,
        shift_two,
        qkv_weight.transpose(1, 0, 2).reshape(3, 4, 2, width // 8, heads_width),
        out_weight.reshape(4, 2, heads_width // 8, width),
        up_weight.reshape(4, 2, width // 8, hidden),
        down_weight.reshape(tiles, 4, 2, TILE // 8, width),
    )
    rest = dp // 16
    if rest > 1:
        groups = [list(range(g * rest, (g + 1) * rest)) for g in range(16)]
        scatter = functools.partial(lax.psum_scatter, axis_name="dp", axis_index_groups=groups, tiled=True)
        qg = scatter(qg, scatter_dimension=1)
        pgt, ug, dgt = (scatter(part, scatter_dimension=0) for part in (pgt, ug, dgt))
        ng = lax.psum(ng, "dp", axis_index_groups=groups)
    share = width // dp
    results = (out, ig, qg, pgt, ug, dgt)
    out, ig, qg, pgt, ug, dgt, ng = pl.pallas_call(
        collect_kernel,
        out_shape=tuple(S(a.shape, a.dtype) for a in results) + (S((4, share), F32),),
        in_specs=[far] * 7,
        out_specs=[far] * 7,
        scratch_shapes=[V(a.shape, a.dtype) for a in results]
        + [V(ng.shape, F32), V((4, share), F32), pltpu.SemaphoreType.DMA((2, 24))],
        name="collect",
    )(*results, ng)
    return out, ig, qg.transpose(1, 0, 2), pgt.T, ug, dgt.T, ng


def solution(mesh):
    in_specs = (
        P("dp", None),
        P("dp"),
        P(),
        P(),
        P(None, None, "tp"),
        P("tp", None),
        P(),
        P(),
        P(None, "tp"),
        P("tp", None),
        P("dp", None),
    )
    out_specs = (
        P("dp", None),
        P("dp", None),
        P("dp", None, "tp"),
        P("tp", "dp"),
        P("dp", "tp"),
        P("tp", "dp"),
        P(None, "dp"),
    )
    step = functools.partial(local, mesh.shape["dp"])
    return jax.shard_map(step, mesh=mesh, in_specs=in_specs, out_specs=out_specs, check_vma=False)
```
